128 devices in a mesh: dp: 16 (over x_hi, y, core), mp: 8 (over x_lo, z).
Axes of the slice: x: 4 (x_hi: 2, x_lo: 2; x = x_hi * 2 + x_lo), y: 4, z: 4, core: 2. Of those that a mesh axis runs over, the one named last changes fastest.
Arguments:
- inputs: bfloat16 [16, 1024, 2048], P('dp', 'mp'), may hold values from -6 to 6
- lengths: int32 [16], P('dp'), may hold values from 256 to 1024, as said below
- head_sizes: int32 [16], P('mp'), may hold values from 170 to 171, as said below
- h_start: float32 [16, 3072], P('dp', 'mp'), may hold values from -4 to 4
- conv_start: float32 [16, 3, 3072], P('dp', None, 'mp'), may hold values from -6 to 6
- g_one: float32 [2048], replicated, may hold values from 0.5 to 1.5
- w_a: bfloat16 [2048, 3072], P('dp', 'mp'), may hold values from -0.125 to 0.125
- w_b: bfloat16 [2048, 3072], P('dp', 'mp'), may hold values from -0.125 to 0.125
- conv_w: float32 [4, 3072], P(None, 'mp'), may hold values from -3 to 3
- conv_b: float32 [3072], P('mp'), may hold values from -2 to 2
- w_r: bfloat16 [16, 192, 192], P('mp'), may hold values from -0.4375 to 0.4375
- w_i: bfloat16 [16, 192, 192], P('mp'), may hold values from -0.4375 to 0.4375
- b_r: float32 [3072], P('mp'), may hold values from -3 to 3
- b_i: float32 [3072], P('mp'), may hold values from -3 to 3
- lam: float32 [3072], P('mp'), may hold values from 3.5 to 10
- w_out: bfloat16 [3072, 2048], P('mp', 'dp'), may hold values from -0.4375 to 0.4375
- g_two: float32 [2048], replicated, may hold values from 0.5 to 1.5
- w_gate: bfloat16 [2048, 6144], P('dp', 'mp'), may hold values from -0.125 to 0.125
- w_up: bfloat16 [2048, 6144], P('dp', 'mp'), may hold values from -0.125 to 0.125
- w_down: bfloat16 [6144, 2048], P('mp', 'dp'), may hold values from -0.15625 to 0.15625
- cotangent: bfloat16 [16, 1024, 2048], P('dp', 'mp'), may hold values from -6 to 6
Outputs:
- result: bfloat16 [16, 1024, 2048], P('dp', 'mp')
- final_h: float32 [16, 3072], P('dp', 'mp')
- final_conv: float32 [16, 3, 3072], P('dp', None, 'mp')
- d_inputs: float32 [16, 1024, 2048], P('dp', 'mp')
- d_g_one: float32 [2048], replicated
- d_w_a: float32 [2048, 3072], P('dp', 'mp')
- d_w_b: float32 [2048, 3072], P('dp', 'mp')
- d_conv_w: float32 [4, 3072], P(None, 'mp')
- d_conv_b: float32 [3072], P('mp')
- d_w_r: float32 [16, 192, 192], P('mp')
- d_w_i: float32 [16, 192, 192], P('mp')
- d_b_r: float32 [3072], P('mp')
- d_b_i: float32 [3072], P('mp')
- d_lam: float32 [3072], P('mp')
- d_w_out: float32 [3072, 2048], P('mp', 'dp')
- d_g_two: float32 [2048], replicated
- d_w_gate: float32 [2048, 6144], P('dp', 'mp')
- d_w_up: float32 [2048, 6144], P('dp', 'mp')
- d_w_down: float32 [6144, 2048], P('mp', 'dp')
The draws below stay inside these ranges and needn't reach their ends.
Inputs may be any that keep to these rules, and one draw needn't show every extreme that they name: `lengths`: half of the rows have length 1024, the others 256. `head_sizes`: 16 * 5 // 8 heads have 171 live channels, the others 171 - 1.
All inputs are finite; a program needn't handle non-finite values.
Results may differ from the reference program's by a relative error of at most 0.015.
Values may be sent and summed in bfloat16 or wider, within the bound.
No kernel may reach another device: no remote copies, remote signals or barrier semaphores. Data moves between devices by JAX's collectives and lax.ppermute only.
A program may use at most 192 MiB of HBM per device.

```python
import jax
import jax.numpy as jnp
from jax import lax

D = 2048
FF = 6144
NHEAD = 16
HEAD_LIVE = 171
HS = 192
SEQ = 1024
SHORT = 256
LW = 3072
ROWS = 16


def draw_lengths(key, part):
    key = jax.random.fold_in(key, 11)
    order = jax.random.permutation(key, ROWS)
    return jnp.where(order < ROWS // 2, SEQ, SHORT).astype(jnp.int32)


def draw_head_sizes(key, part):
    key = jax.random.fold_in(key, 23)
    order = jax.random.permutation(key, NHEAD)
    return jnp.where(order < NHEAD * 5 // 8, HEAD_LIVE, HEAD_LIVE - 1).astype(jnp.int32)


def level_of(rng, shape, shards, smallest, high):
    level, own = 1.0, jax.random.fold_in(rng, 6)
    for position, shards_of in shards:
        steps = jnp.exp(jax.random.uniform(jax.random.fold_in(own, position), (shards_of,), jnp.float32, smallest / len(shards), high / len(shards)))
        level = level * jnp.repeat(steps, shape[position] // shards_of).reshape([-1 if axis == position else 1 for axis in range(len(shape))])
    return level


def scatter_about(stream_key, dims, width, bound, cuts=(), held_as=jnp.bfloat16):
    values = width * jax.random.normal(stream_key, dims, jnp.float32)
    if cuts:
        values = values * level_of(stream_key, dims, cuts, -0.22, 0.18)
    return jnp.clip(values, -bound, bound).astype(held_as)


def setup_inputs(seed: int = 0) -> dict:
    key_list = jax.random.split(jax.random.key(seed), 22)
    return {
        "inputs": scatter_about(key_list[0], (ROWS, SEQ, D), 1.0, 6.0, ((0, 16), (1, 8))),
        "lengths": draw_lengths(jax.random.fold_in(key_list[21], 71), 0),
        "head_sizes": draw_head_sizes(jax.random.fold_in(key_list[21], 71), 0),
        "h_start": scatter_about(key_list[3], (ROWS, LW), 0.5, 4.0, ((0, 16), (1, 8)), jnp.float32),
        "conv_start": scatter_about(key_list[4], (ROWS, 3, LW), 1.0, 6.0, ((0, 16), (2, 8)), jnp.float32),
        "g_one": jnp.clip(1.0 + 0.1 * jax.random.normal(key_list[5], (D,), jnp.float32), 0.5, 1.5),
        "w_a": scatter_about(key_list[6], (D, LW), D ** -0.5, 0.125, ((0, 16), (1, 8))),
        "w_b": scatter_about(key_list[7], (D, LW), D ** -0.5, 0.125, ((0, 16), (1, 8))),
        "conv_w": scatter_about(key_list[8], (4, LW), 4 ** -0.5, 3.0, ((1, 8),), jnp.float32),
        "conv_b": scatter_about(key_list[9], (LW,), 0.3, 2.0, ((0, 8),), jnp.float32),
        "w_r": scatter_about(key_list[10], (NHEAD, HS, HS), HS ** -0.5, 0.4375, ((0, 8),)),
        "w_i": scatter_about(key_list[11], (NHEAD, HS, HS), HS ** -0.5, 0.4375, ((0, 8),)),
        "b_r": scatter_about(key_list[12], (LW,), 0.5, 3.0, ((0, 8),), jnp.float32),
        "b_i": scatter_about(key_list[13], (LW,), 0.5, 3.0, ((0, 8),), jnp.float32),
        "lam": jnp.clip(3.5 + 6.5 * jax.random.uniform(key_list[14], (LW,), jnp.float32) ** level_of(key_list[14], (LW,), ((0, 8),), -0.2, 0.2), 3.5, 10.0),
        "w_out": scatter_about(key_list[15], (LW, D), (LW // 16) ** -0.5, 0.4375, ((0, 8), (1, 16))),
        "g_two": jnp.clip(1.0 + 0.1 * jax.random.normal(key_list[16], (D,), jnp.float32), 0.5, 1.5),
        "w_gate": scatter_about(key_list[17], (D, FF), D ** -0.5, 0.125, ((0, 16), (1, 8))),
        "w_up": scatter_about(key_list[18], (D, FF), D ** -0.5, 0.125, ((0, 16), (1, 8))),
        "w_down": scatter_about(key_list[19], (FF, D), (FF // 4) ** -0.5, 0.15625, ((0, 8), (1, 16))),
        "cotangent": scatter_about(key_list[20], (ROWS, SEQ, D), 1.0, 6.0, ((0, 16), (1, 8))),
    }


@jax.custom_vjp
def low(v):
    return lax.optimization_barrier(v.astype(jnp.bfloat16)).astype(jnp.float32)

@jax.custom_vjp
def low_back(v):
    return v

def low_keep(v):
    return (low(v), None)

def low_pass(kept, grad):
    return (grad,)

def back_keep(v):
    return (v, None)

def back_low(kept, grad):
    return (low(grad),)
low.defvjp(low_keep, low_pass)
low_back.defvjp(back_keep, back_low)
EPS = 1e-06
HIGH = lax.Precision.HIGHEST

def project(operand, weights):
    return jnp.einsum('rtd,de->rte', operand, weights, precision=HIGH)

def rms_norm(values, gains):
    return values * lax.rsqrt(lax.optimization_barrier(jnp.mean(values * values, axis=-1, keepdims=True)) + EPS) * gains

def linear_step(carry, pair):
    carry = pair[0] * carry + pair[1]
    return (carry, carry)

def window_end(extended_row, length_one):
    return lax.dynamic_slice_in_dim(extended_row, length_one.astype(jnp.int32), 3, 0)

def block_forward(values, lengths, channel_mask, h_start, conv_start, g_one, w_a, w_b, conv_w, conv_b, w_r, w_i, b_r, b_i, lam, w_out, g_two, w_gate, w_up, w_down):
    row_count, step_count = (values.shape[0], values.shape[1])
    n_one = low(rms_norm(values, g_one))
    pre_a = low_back(project(n_one, w_a))
    pre_b = low_back(project(n_one, w_b)) * channel_mask
    extended = jnp.concatenate([conv_start * channel_mask, pre_b], axis=1)
    conv_out = conv_b + conv_w[0] * extended[:, 0:step_count]
    for offset in range(1, 4):
        conv_out = conv_out + conv_w[offset] * extended[:, offset:offset + step_count]
    conv_out = conv_out * channel_mask
    heads_in = low(conv_out).reshape(row_count, step_count, NHEAD, HS)
    pre_r = low_back(jnp.einsum('rthi,hij->rthj', heads_in, w_r, precision=HIGH).reshape(row_count, step_count, LW) + b_r)
    pre_i = low_back(jnp.einsum('rthi,hij->rthj', heads_in, w_i, precision=HIGH).reshape(row_count, step_count, LW) + b_i)
    recur_gate = jax.nn.sigmoid(pre_r)
    input_gate = jax.nn.sigmoid(pre_i)
    log_decay = -8.0 * recur_gate * jax.nn.softplus(-lam)
    decay_rate = jnp.exp(log_decay)
    multiplier = jnp.sqrt(-jnp.expm1(2.0 * log_decay))
    valid_mask = (jnp.arange(step_count)[None, :] < lengths[:, None])[:, :, None]
    decay_used = jnp.where(valid_mask, decay_rate, 1.0)
    drive_term = jnp.where(valid_mask, multiplier * input_gate * conv_out, 0.0)
    last_state, states = lax.scan(linear_step, h_start * channel_mask, (jnp.swapaxes(decay_used, 0, 1), jnp.swapaxes(drive_term, 0, 1)))
    states = jnp.swapaxes(states, 0, 1)
    mixer_in = low(jax.nn.gelu(pre_a) * states)
    x_one = values + low_back(project(mixer_in, w_out))
    n_two = low(rms_norm(x_one, g_two))
    gate_pre = low_back(project(n_two, w_gate))
    up_pre = low_back(project(n_two, w_up))
    hidden = low(jax.nn.gelu(gate_pre) * up_pre)
    result = x_one + low_back(project(hidden, w_down))
    conv_end = jax.vmap(window_end)(extended, lengths)
    return (result, (last_state, conv_end))

def reference(inputs, lengths, head_sizes, h_start, conv_start, g_one, w_a, w_b, conv_w, conv_b, w_r, w_i, b_r, b_i, lam, w_out, g_two, w_gate, w_up, w_down, cotangent):
    channel_mask = (jnp.arange(HS)[None, :] < head_sizes[:, None]).astype(jnp.float32).reshape(LW)
    params = tuple((weight.astype(jnp.float32) for weight in (g_one, w_a, w_b, conv_w, conv_b, w_r, w_i, b_r, b_i, lam, w_out, g_two, w_gate, w_up, w_down)))
    group_total = ROWS // 4

    def regroup(array):
        return array.reshape((group_total, 4) + array.shape[1:])

    def one_group(totals, group_items):
        x_group, len_group, h_group, c_group, cot_group = group_items

        def group_block(x_value, *weights):
            return block_forward(x_value, len_group, channel_mask, h_group, c_group, *weights)
        block_out, pullback, extras = jax.vjp(group_block, x_group.astype(jnp.float32), *params, has_aux=True)
        gradients = pullback(cot_group.astype(jnp.float32))
        totals = tuple((total + gradient for total, gradient in zip(totals, gradients[1:])))
        return (totals, (block_out.astype(jnp.bfloat16), extras[0], extras[1], gradients[0]))
    zero_grads = tuple((jnp.zeros_like(weight) for weight in params))
    totals, stacked = lax.scan(one_group, zero_grads, (regroup(inputs), regroup(lengths), regroup(h_start), regroup(conv_start), regroup(cotangent)))

    def ungroup(array):
        return array.reshape((ROWS,) + array.shape[2:])
    return (ungroup(stacked[0]), ungroup(stacked[1]), ungroup(stacked[2]), ungroup(stacked[3]), totals[0], totals[1], totals[2], totals[3], totals[4], totals[5], totals[6], totals[7], totals[8], totals[9], totals[10], totals[11], totals[12], totals[13], totals[14])
```

```python
import functools

import jax
import jax.numpy as jnp
from jax import lax
from jax.experimental import pallas as pl
from jax.experimental.pallas import tpu as pltpu
from jax.sharding import PartitionSpec as P

EPS = 1e-06
F32 = jnp.float32
BF16 = jnp.bfloat16
AXES = ("dp", "mp")
DEVICES = 128

Z_MASKS = (0, 1, 2, 3)
X_MASKS = (0, 4, 64, 68)
Y_MASKS = (0, 16, 32, 48)
CORE = 8
HALF_SEQ = 512
TOK = 128
CH = 384
WIDE = 768
CHUNKS = 8
STEPS = 64
GELU_A = 0.7978845608028654
GELU_B = 0.044715


def swap_send(values, mask):
    return lax.ppermute(values, AXES, [(i, i ^ mask) for i in range(DEVICES)])


def block_of(position, dp):
    mirrored = (position & 6) | ((position & 1) << 3) | ((position >> 3) & 1)
    return dp ^ mirrored


def gelu_parts(v):
    inner = GELU_A * (v + GELU_B * v * v * v)
    t = jnp.tanh(inner)
    half = 0.5 * (1.0 + t)
    slope = half + 0.5 * v * (1.0 - t * t) * (GELU_A * (1.0 + (3.0 * GELU_B) * v * v))
    return v * half, slope


def gelu_value(v):
    return v * (0.5 * (1.0 + jnp.tanh(GELU_A * (v + GELU_B * v * v * v))))


def neg_expm1(v):
    series = 1.0 + v * (1.0 / 9.0)
    for n in range(8, 1, -1):
        series = 1.0 + (v * (1.0 / n)) * series
    return jnp.where(v > -0.5, -v * series, 1.0 - jnp.exp(v))


def vmem(limit):
    return pltpu.CompilerParams(vmem_limit_bytes=limit * 1024 * 1024)


SMEM_SPEC = pl.BlockSpec(memory_space=pltpu.SMEM)


def prep_kernel(scal, x_ref, c_ref, g1_ref, g2_ref, xr_ref, n1_ref, cr_ref, g1r_ref, g2r_ref):
    dp = scal[2]
    total = jnp.zeros((TOK, 128), F32)
    for p in range(16):
        src = pl.ds(pl.multiple_of(block_of(p, dp) * 128, 128), 128)
        dst = slice(p * 128, (p + 1) * 128)
        xb = x_ref[:, src]
        xr_ref[:, dst] = xb
        cr_ref[:, dst] = c_ref[:, src]
        g1r_ref[:, dst] = g1_ref[:, src]
        g2r_ref[:, dst] = g2_ref[:, src]
        xf = xb.astype(F32)
        total = total + xf * xf
    s = lax.rsqrt(jnp.sum(total, axis=-1, keepdims=True) * (1.0 / 2048.0) + EPS)
    n1_ref[...] = (xr_ref[...].astype(F32) * s * g1r_ref[...]).astype(BF16)


def prep(scal, x, c, g1, g2):
    return pl.pallas_call(
        prep_kernel,
        out_shape=(
            jax.ShapeDtypeStruct((TOK, 2048), BF16),
            jax.ShapeDtypeStruct((TOK, 2048), BF16),
            jax.ShapeDtypeStruct((TOK, 2048), BF16),
            jax.ShapeDtypeStruct((1, 2048), F32),
            jax.ShapeDtypeStruct((1, 2048), F32),
        ),
        in_specs=[SMEM_SPEC] + [pl.BlockSpec(memory_space=pltpu.VMEM)] * 4,
        compiler_params=vmem(16),
        name="prep",
    )(scal, x, c, g1, g2)


def mid_kernel(x_ref, own0, own1, a0, a1, b0, b1, g_ref, xo_ref, n_ref):
    for h, (own, a, b) in enumerate(((own0, a0, b0), (own1, a1, b1))):
        cols = slice(h * 1024, (h + 1) * 1024)
        xo_ref[:, cols] = x_ref[:, cols].astype(F32) + (
            own[...] + a[...].astype(F32) + b[...].astype(F32)
        )
    x = xo_ref[...]
    s = lax.rsqrt(jnp.mean(x * x, axis=-1, keepdims=True) + EPS)
    n_ref[...] = (x * s * g_ref[...]).astype(BF16)


def mid_norm(x_rel, sums, g):
    (own0, a0, b0), (own1, a1, b1) = sums
    return pl.pallas_call(
        mid_kernel,
        out_shape=(
            jax.ShapeDtypeStruct((TOK, 2048), F32),
            jax.ShapeDtypeStruct((TOK, 2048), BF16),
        ),
        compiler_params=vmem(16),
        name="mid_norm",
    )(x_rel, own0, own1, a0, a1, b0, b1, g)


def back_kernel(scal, base_ref, x_ref, own0, own1, a0, a1, b0, b1, g_ref, *outs, last):
    dn_ref = outs[-1]
    for h, (own, a, b) in enumerate(((own0, a0, b0), (own1, a1, b1))):
        cols = slice(h * 1024, (h + 1) * 1024)
        dn_ref[:, cols] = own[...] + a[...].astype(F32) + b[...].astype(F32)
    x = x_ref[...].astype(F32)
    s = lax.rsqrt(jnp.mean(x * x, axis=-1, keepdims=True) + EPS)
    dn = dn_ref[...]
    w = g_ref[...] * dn
    inner = jnp.mean(w * x, axis=-1, keepdims=True)
    dx = base_ref[...].astype(F32) + s * (w - x * (s * s * inner))
    dg = jnp.sum(dn * x * s, axis=0, keepdims=True)
    dp = scal[2]
    if last:
        dx_ref, dg_ref = outs[:2]
    else:
        dx_ref, dm_ref, dg_ref = outs[:3]
        dx_ref[...] = dx
        dm_ref[...] = dx.astype(BF16)
    for p in range(16):
        dst = pl.ds(pl.multiple_of(block_of(p, dp) * 128, 128), 128)
        cols = slice(p * 128, (p + 1) * 128)
        dg_ref[:, dst] = dg[:, cols]
        if last:
            dx_ref[:, dst] = dx[:, cols]


def norm_back(scal, base, x, sums, g, last):
    (own0, a0, b0), (own1, a1, b1) = sums
    outs = [jax.ShapeDtypeStruct((TOK, 2048), F32)]
    if not last:
        outs.append(jax.ShapeDtypeStruct((TOK, 2048), BF16))
    outs.append(jax.ShapeDtypeStruct((1, 2048), F32))
    return pl.pallas_call(
        functools.partial(back_kernel, last=last),
        out_shape=tuple(outs),
        in_specs=[SMEM_SPEC] + [pl.BlockSpec(memory_space=pltpu.VMEM)] * 9,
        scratch_shapes=[pltpu.VMEM((TOK, 2048), F32)],
        compiler_params=vmem(24),
        name="norm_back",
    )(scal, base, x, own0, own1, a0, a1, b0, b1, g)


def result_kernel(scal, x_ref, own0, own1, a0, a1, b0, b1, out_ref):
    dp = scal[2]
    for p in range(16):
        own, a, b = ((own0, a0, b0), (own1, a1, b1))[p // 8]
        cols = slice((p % 8) * 128, (p % 8) * 128 + 128)
        dst = pl.ds(pl.multiple_of(block_of(p, dp) * 128, 128), 128)
        total = own[:, cols] + a[:, cols].astype(F32) + b[:, cols].astype(F32)
        out_ref[:, dst] = (x_ref[:, p * 128 : (p + 1) * 128] + total).astype(BF16)


def result_sum(scal, x_one, sums):
    (own0, a0, b0), (own1, a1, b1) = sums
    return pl.pallas_call(
        result_kernel,
        out_shape=jax.ShapeDtypeStruct((TOK, 2048), BF16),
        in_specs=[SMEM_SPEC] + [pl.BlockSpec(memory_space=pltpu.VMEM)] * 7,
        compiler_params=vmem(16),
        name="result_sum",
    )(scal, x_one, own0, own1, a0, a1, b0, b1)


ROW_CB, ROW_BR, ROW_BI, ROW_DECAY, ROW_MASK, ROW_H, ROW_SIG = 4, 5, 6, 7, 8, 9, 10


def row(ref, i):
    return ref[i : i + 1, :]


def rel_rows(z, start, size):
    block, inside = start // TOK, start % TOK
    return pl.ds(pl.multiple_of((z ^ block) * TOK + inside, size), size)


def valid_rows(scal, start, size):
    t = lax.broadcasted_iota(jnp.int32, (size, 1), 0) + (scal[1] * HALF_SEQ + start)
    return t < scal[3]


GROUPS = 3


def put(ref, rows, value):
    for g in range(GROUPS):
        ref[g, rows, :] = value[:, g * 128 : (g + 1) * 128]


def take(ref, rows):
    return jnp.concatenate([ref[g, rows, :] for g in range(GROUPS)], axis=1)


def at_step(ref, s):
    rows = pl.ds(s, CHUNKS, stride=STEPS)
    return [ref.at[g][rows, :] for g in range(GROUPS)]


def put_step(ref, s, values):
    rows = pl.ds(s, CHUNKS, stride=STEPS)
    for g in range(GROUPS):
        ref.at[g][rows, :] = values[g]


def run_steps(step):
    start = [jnp.zeros((CHUNKS, 128), F32)] * GROUPS + [jnp.ones((CHUNKS, 128), F32)] * GROUPS
    out = lax.fori_loop(0, STEPS, step, tuple(start), unroll=4)
    return jnp.concatenate(out[:GROUPS], axis=1), jnp.concatenate(out[GROUPS:], axis=1)


def mix_fwd_kernel(
    scal, pre_b, halo, par, wr, wi, rate, inlet, conv, xg, av, hl, pcum, ext, end, bv
):
    z = scal[0]
    mask = row(par, ROW_MASK)
    ext[0:8, :] = halo[...]
    for c in range(CHUNKS):
        ext[8 + c * STEPS : 8 + (c + 1) * STEPS, :] = pre_b[rel_rows(z, c * STEPS, STEPS), :] * mask
    for c in range(CHUNKS):
        t0 = c * STEPS
        acc = row(par, ROW_CB) + row(par, 0) * ext[t0 + 5 : t0 + 5 + STEPS, :]
        for k in range(1, 4):
            acc = acc + row(par, k) * ext[t0 + 5 + k : t0 + 5 + k + STEPS, :]
        acc = acc * mask
        conv[t0 : t0 + STEPS, :] = acc
        xg[t0 : t0 + STEPS, :] = acc.astype(BF16)
    rate[...] = jnp.dot(xg[...], wr[0], preferred_element_type=F32)
    inlet[...] = jnp.dot(xg[...], wi[0], preferred_element_type=F32)
    for c in range(CHUNKS):
        rows = slice(c * STEPS, (c + 1) * STEPS)
        r = jax.nn.sigmoid(rate[rows, :] + row(par, ROW_BR))
        i = jax.nn.sigmoid(inlet[rows, :] + row(par, ROW_BI))
        rate[rows, :] = r
        inlet[rows, :] = i
        log_a = row(par, ROW_DECAY) * r
        mult = jnp.sqrt(neg_expm1(2.0 * log_a))
        valid = valid_rows(scal, c * STEPS, STEPS)
        put(av, rows, jnp.where(valid, jnp.exp(log_a), 1.0))
        put(bv, rows, jnp.where(valid, mult * i * conv[rows, :], 0.0))

    def step(s, carry):
        a, b = at_step(av, s), at_step(bv, s)
        h = [a[g] * carry[g] + b[g] for g in range(GROUPS)]
        p = [a[g] * carry[GROUPS + g] for g in range(GROUPS)]
        put_step(hl, s, h)
        put_step(pcum, s, p)
        return tuple(h + p)

    h, p = run_steps(step)
    carry = row(par, ROW_H)
    for c in range(CHUNKS):
        carry = h[c : c + 1, :] + p[c : c + 1, :] * carry
    end[...] = jnp.broadcast_to(carry, (8, CH))


def wide(rows):
    return pl.BlockSpec((rows, CH), lambda i: (0, i))


GATE_SPEC = pl.BlockSpec((1, CH, CH), lambda i: (i, 0, 0))


STRIP_SPEC = pl.BlockSpec((GROUPS, 512, 128), lambda i: (i, 0, 0))
STRIP = jax.ShapeDtypeStruct((2 * GROUPS, 512, 128), F32)
STRIP_SCRATCH = pltpu.VMEM((GROUPS, 512, 128), F32)


def sds(rows, dtype=F32):
    return jax.ShapeDtypeStruct((rows, WIDE), dtype)


def mix_fwd(scal, pre_b, halo, par, wr, wi):
    return pl.pallas_call(
        mix_fwd_kernel,
        grid=(2,),
        out_shape=(
            sds(512), sds(512), sds(512), sds(512, BF16), STRIP, STRIP, STRIP, sds(520), sds(8),
        ),
        in_specs=[SMEM_SPEC, wide(512), wide(8), wide(16), GATE_SPEC, GATE_SPEC],
        out_specs=(
            wide(512), wide(512), wide(512), wide(512), STRIP_SPEC, STRIP_SPEC, STRIP_SPEC, wide(520), wide(8),
        ),
        scratch_shapes=[STRIP_SCRATCH],
        compiler_params=vmem(32),
        name="mix_fwd",
    )(scal, pre_b, halo, par, wr, wi)


def mix_out_kernel(scal, hl, pcum, pre_a, h_in, h_ext, mixed, final):
    z = scal[0]
    h_ext[0:8, :] = h_in[...]
    carry = row(h_in, 7)
    for c in range(CHUNKS):
        rows = slice(c * STEPS, (c + 1) * STEPS)
        h = take(hl, rows) + take(pcum, rows) * carry
        h_ext[8 + c * STEPS : 8 + (c + 1) * STEPS, :] = h
        carry = h[STEPS - 1 : STEPS, :]
        rel = rel_rows(z, c * STEPS, STEPS)
        mixed[rel, :] = (gelu_value(pre_a[rel, :]) * h).astype(BF16)
    final[...] = jnp.broadcast_to(carry, (8, CH))


def mix_out(scal, hl, pcum, pre_a, h_in):
    return pl.pallas_call(
        mix_out_kernel,
        grid=(2,),
        out_shape=(sds(520), sds(512, BF16), sds(8)),
        in_specs=[SMEM_SPEC, STRIP_SPEC, STRIP_SPEC, wide(512), wide(8)],
        out_specs=(wide(520), wide(512), wide(8)),
        compiler_params=vmem(32),
        name="mix_out",
    )(scal, hl, pcum, pre_a, h_in)


def mix_back_kernel(scal, d_mix, pre_a, h_ext, av, d_pre_a, rl, qcum, end, dh):
    z = scal[0]
    for c in range(CHUNKS):
        rel = rel_rows(z, c * STEPS, STEPS)
        act, slope = gelu_parts(pre_a[rel, :])
        dm = d_mix[rel, :]
        h = h_ext[8 + c * STEPS : 8 + (c + 1) * STEPS, :]
        d_pre_a[rel, :] = (slope * h * dm).astype(BF16)
        put(dh, slice(c * STEPS, (c + 1) * STEPS), dm * act)

    def step(n, carry):
        s = STEPS - 1 - n
        a, d = at_step(av, s), at_step(dh, s)
        carried = [d[g] + carry[g] for g in range(GROUPS)]
        put_step(rl, s, carried)
        put_step(qcum, s, carry[GROUPS:])
        u = [a[g] * carried[g] for g in range(GROUPS)]
        return tuple(u + [a[g] * carry[GROUPS + g] for g in range(GROUPS)])

    u, q = run_steps(step)
    carry = jnp.zeros((1, CH), F32)
    for c in range(CHUNKS - 1, -1, -1):
        carry = u[c : c + 1, :] + q[c : c + 1, :] * carry
    end[...] = jnp.broadcast_to(carry, (8, CH))


def mix_back(scal, d_mix, pre_a, h_ext, av):
    return pl.pallas_call(
        mix_back_kernel,
        grid=(2,),
        out_shape=(sds(512, BF16), STRIP, STRIP, sds(8)),
        in_specs=[SMEM_SPEC, wide(512), wide(512), wide(520), STRIP_SPEC],
        out_specs=(wide(512), STRIP_SPEC, STRIP_SPEC, wide(8)),
        scratch_shapes=[STRIP_SCRATCH],
        compiler_params=vmem(32),
        name="mix_back",
    )(scal, d_mix, pre_a, h_ext, av)


def total_rows(v):
    return jnp.sum(v, axis=0, keepdims=True)


def mix_grad_kernel(
    scal, rl, qcum, av, u_in, rate, inlet, conv, h_ext, ext, par, wr, wi,
    d_pre_r, d_pre_i, d_pre_b, tail, head, sums, dconv,
):
    z = scal[0]
    mask = row(par, ROW_MASK)
    carry = row(u_in, 0)
    d_lam = jnp.zeros((1, CH), F32)
    d_br = jnp.zeros((1, CH), F32)
    d_bi = jnp.zeros((1, CH), F32)
    for c in range(CHUNKS - 1, -1, -1):
        t0 = c * STEPS
        rows = slice(t0, t0 + STEPS)
        a = take(av, rows)
        carried = take(rl, rows) + take(qcum, rows) * carry
        carry = a[0:1, :] * carried[0:1, :]
        valid = valid_rows(scal, t0, STEPS)
        d_drive = jnp.where(valid, carried, 0.0)
        d_decay = d_drive * h_ext[t0 + 7 : t0 + 7 + STEPS, :]
        r, i, x = rate[rows, :], inlet[rows, :], conv[rows, :]
        gap = neg_expm1(2.0 * (row(par, ROW_DECAY) * r))
        inv = lax.rsqrt(gap)
        mult = gap * inv
        driven = d_drive * i
        d_log = d_decay * a - driven * x * (a * a) * inv
        d_lam = d_lam + total_rows(d_log * r)
        pr = (d_log * row(par, ROW_DECAY) * r * (1.0 - r)).astype(BF16)
        pi = (d_drive * mult * x * i * (1.0 - i)).astype(BF16)
        d_pre_r[rows, :] = pr
        d_pre_i[rows, :] = pi
        d_br = d_br + total_rows(pr.astype(F32))
        d_bi = d_bi + total_rows(pi.astype(F32))
        dconv[rows, :] = driven * mult
    dims = (((1,), (1,)), ((), ()))
    gate = lax.dot_general(d_pre_r[...], wr[0], dims, preferred_element_type=F32)
    gate = gate + lax.dot_general(d_pre_i[...], wi[0], dims, preferred_element_type=F32)
    dconv[0:HALF_SEQ, :] = (dconv[0:HALF_SEQ, :] + gate) * mask
    dconv[HALF_SEQ : HALF_SEQ + 8, :] = jnp.zeros((8, CH), F32)
    head[...] = dconv[0:8, :]
    taps = [jnp.zeros((1, CH), F32) for _ in range(4)]
    bias = jnp.zeros((1, CH), F32)
    for c in range(CHUNKS):
        t0 = c * STEPS
        here = dconv[t0 : t0 + STEPS, :]
        bias = bias + total_rows(here)
        back = jnp.zeros((STEPS, CH), F32)
        for k in range(4):
            taps[k] = taps[k] + total_rows(here * ext[t0 + 5 + k : t0 + 5 + k + STEPS, :])
            back = back + row(par, k) * dconv[t0 + 3 - k : t0 + 3 - k + STEPS, :]
        back = back * mask
        d_pre_b[rel_rows(z, t0, STEPS), :] = back.astype(BF16)
        if c == CHUNKS - 1:
            tail[...] = back[STEPS - 16 :, :]
    for k in range(4):
        sums[k : k + 1, :] = taps[k]
    sums[4:5, :] = bias
    sums[5:6, :] = d_br
    sums[6:7, :] = d_bi
    sums[7:8, :] = 8.0 * row(par, ROW_SIG) * d_lam


def mix_grad(scal, rl, qcum, av, u_in, rate, inlet, conv, h_ext, ext, par, wr, wi):
    return pl.pallas_call(
        mix_grad_kernel,
        grid=(2,),
        out_shape=(sds(512, BF16), sds(512, BF16), sds(512, BF16), sds(16), sds(8), sds(8)),
        in_specs=[
            SMEM_SPEC, STRIP_SPEC, STRIP_SPEC, STRIP_SPEC, wide(8), wide(512), wide(512), wide(512),
            wide(520), wide(520), wide(16), GATE_SPEC, GATE_SPEC,
        ],
        out_specs=(wide(512), wide(512), wide(512), wide(16), wide(8), wide(8)),
        scratch_shapes=[pltpu.VMEM((HALF_SEQ + 8, CH), F32)],
        compiler_params=vmem(40),
        name="mix_grad",
    )(scal, rl, qcum, av, u_in, rate, inlet, conv, h_ext, ext, par, wr, wi)


def gather_z(halves):
    h0, h1 = halves
    p3_0 = swap_send(h0, 3)
    p1_1 = swap_send(h1, 1)
    p3_1 = swap_send(h1, 3)
    p1_0 = swap_send(h0, 1)
    p2_0 = swap_send(p3_0, 1)
    p2_1 = swap_send(p1_1, 3)
    return (
        jnp.concatenate([h0, p1_0, p2_0, p3_0], axis=0),
        jnp.concatenate([h1, p1_1, p2_1, p3_1], axis=0),
    )


def scatter_z(part0, part1):
    def block(part, j):
        return part[j * TOK : (j + 1) * TOK]

    far_0 = swap_send(block(part0, 2).astype(BF16), 1)
    far_1 = swap_send(block(part1, 2).astype(BF16), 3)
    r1_0 = swap_send(block(part0, 1).astype(BF16), 1)
    r3_1 = swap_send(block(part1, 3).astype(BF16), 3)
    r1_1 = swap_send((block(part1, 1) + far_1.astype(F32)).astype(BF16), 1)
    r3_0 = swap_send((block(part0, 3) + far_0.astype(F32)).astype(BF16), 3)
    return (block(part0, 0), r1_0, r3_0), (block(part1, 0), r1_1, r3_1)


def cross(rows_of, blocks):
    return jnp.concatenate(
        [
            jnp.concatenate([blocks[0], blocks[1]], axis=-1),
            jnp.concatenate([blocks[2], blocks[3]], axis=-1),
        ],
        axis=rows_of,
    )


def gather_xy(shard):
    rows = cross(0, [shard] + [swap_send(shard, m) for m in X_MASKS[1:]])
    mine = jnp.concatenate([rows] + [swap_send(rows, m) for m in Y_MASKS[1:]], axis=0)
    return mine


def gather_yx(shard):
    n = shard.shape[1]
    rows = jnp.stack([shard] + [swap_send(shard, m) for m in Y_MASKS[1:]], axis=0)
    blocks = [rows] + [swap_send(rows, m) for m in X_MASKS[1:]]
    return cross(1, blocks).reshape(1024, 2 * n)


def with_core(mine):
    return mine, swap_send(mine, CORE)


def sum_four(own, received):
    a, b, c = [r.astype(F32) for r in received]
    return (own + a) + (b + c)


def scatter_core(mine, other):
    return mine + swap_send(other.astype(BF16), CORE).astype(F32)


def x_pieces(total):
    n = total.shape[-1] // 2
    return [total[:, r * 128 : (r + 1) * 128, c * n : (c + 1) * n] for r in (0, 1) for c in (0, 1)]


def scatter_yx(total):
    n = total.shape[1]
    blocks = total.reshape(4, 256, n)
    rows = sum_four(
        blocks[0], [swap_send(blocks[k].astype(BF16), Y_MASKS[k]) for k in (1, 2, 3)]
    )
    pieces = x_pieces(rows[None])
    return sum_four(
        pieces[0], [swap_send(pieces[k].astype(BF16), X_MASKS[k]) for k in (1, 2, 3)]
    )[0]


def scatter_xy(total):
    n = total.shape[1]
    pieces = x_pieces(total.reshape(4, 256, n))
    rows = sum_four(
        pieces[0], [swap_send(pieces[k].astype(BF16), X_MASKS[k]) for k in (1, 2, 3)]
    )
    return sum_four(rows[0], [swap_send(rows[k].astype(BF16), Y_MASKS[k]) for k in (1, 2, 3)])


def all_sum(values, masks):
    a, b, c = [swap_send(values, m).astype(F32) for m in masks[1:]]
    return (values.astype(F32) + a) + (b + c)


def swap_channels(v):
    return jnp.concatenate([v[..., CH:], v[..., :CH]], axis=-1)


def dot(a, b):
    return jnp.dot(a, b, preferred_element_type=F32)


def dot_back(a, b):
    return lax.dot_general(a, b, (((1,), (1,)), ((), ())), preferred_element_type=F32)


def dot_outer(a, b):
    return lax.dot_general(a, b, (((0,), (0,)), ((), ())), preferred_element_type=F32)


def dot_pair(rows, weights):
    return dot(rows[0], weights[0]) + dot(rows[1], weights[1])


def halves_of(v):
    return v[:, :1024], v[:, 1024:]


def pair_blocks(w):
    hs = w.shape[1]
    zero = jnp.zeros((hs, hs), w.dtype)
    return jnp.concatenate(
        [jnp.concatenate([w[0], zero], axis=1), jnp.concatenate([zero, w[1]], axis=1)], axis=0
    )


def on_device(
    inputs,
    lengths,
    head_sizes,
    h_start,
    conv_start,
    g_one,
    w_a,
    w_b,
    conv_w,
    conv_b,
    w_r,
    w_i,
    b_r,
    b_i,
    lam,
    w_out,
    g_two,
    w_gate,
    w_up,
    w_down,
    cotangent,
):
    dp = lax.axis_index("dp").astype(jnp.int32)
    mp = lax.axis_index("mp").astype(jnp.int32)
    z, x_lo = mp % 4, mp // 4
    length = lengths[0]
    scal = jnp.stack([z, x_lo, dp, length])
    first_half = x_lo == 0

    channel_mask = (
        (jnp.arange(192)[None, :] < head_sizes[:, None]).astype(F32).reshape(1, CH)
    )
    pack = jnp.concatenate(
        [
            conv_w,
            conv_b[None],
            b_r[None],
            b_i[None],
            -8.0 * jax.nn.softplus(-lam)[None],
            channel_mask,
            h_start * channel_mask,
            jax.nn.sigmoid(-lam)[None],
            conv_start[0] * channel_mask,
            jnp.zeros((2, CH), F32),
        ],
        axis=0,
    )
    par = jnp.concatenate([pack, swap_send(pack, 4)], axis=1)
    gates = jnp.stack([pair_blocks(w_r), pair_blocks(w_i)])
    gates = jnp.stack([gates, swap_send(gates, 4)], axis=1)
    wr, wi = gates[0], gates[1]

    x_rel, n_one, c_rel, g_one_rel, g_two_rel = prep(
        scal, inputs[0], cotangent[0], g_one[None], g_two[None]
    )
    rows_one = gather_z(halves_of(n_one))
    wa = with_core(gather_xy(w_a))
    wb = with_core(gather_yx(w_b))
    wo = with_core(gather_yx(w_out.T))
    wg = with_core(gather_xy(w_gate))
    wu = with_core(gather_yx(w_up))
    wd = with_core(gather_xy(w_down.T))

    pre_b = dot_pair(rows_one, wb)
    edge = lax.dynamic_slice_in_dim(pre_b, (z ^ 3) * TOK + TOK - 8, 8, 0)
    edge = swap_channels(swap_send(edge, 4)) * par[ROW_MASK : ROW_MASK + 1]
    start_halo = jnp.concatenate([jnp.zeros((5, WIDE), F32), par[11:14]], axis=0)
    halo = jnp.where(first_half, start_halo, edge)
    par_used = par.at[ROW_H].set(jnp.where(first_half, par[ROW_H], 0.0))
    pre_a = dot_pair(rows_one, wa)
    rate, inlet, conv, xg, av, hl, pcum, ext, end = mix_fwd(scal, pre_b, halo, par_used, wr, wi)
    arrived = swap_channels(swap_send(end, 4))
    h_in = jnp.where(first_half, jnp.broadcast_to(par[ROW_H : ROW_H + 1], (8, WIDE)), arrived)
    rows_c = gather_z(halves_of(c_rel))
    d_hidden = dot_pair(rows_c, wd)
    h_ext, mixer_in, final = mix_out(scal, hl, pcum, pre_a, h_in)

    sums = scatter_z(dot_back(mixer_in, wo[0]), dot_back(mixer_in, wo[1]))
    x_one, n_two = mid_norm(x_rel, sums, g_two_rel)

    rows_two = gather_z(halves_of(n_two))
    gate_pre = dot_pair(rows_two, wg)
    up_pre = dot_pair(rows_two, wu)
    act, slope = gelu_parts(gate_pre)
    hidden = (act * up_pre).astype(BF16)
    d_gate = (slope * (up_pre * d_hidden)).astype(BF16)
    d_up = (act * d_hidden).astype(BF16)
    sums = scatter_z(
        dot_back(d_gate, wg[0]) + dot_back(d_up, wu[0]),
        dot_back(d_gate, wg[1]) + dot_back(d_up, wu[1]),
    )
    d_x_one, dm, d_g_two = norm_back(scal, c_rel, x_one, sums, g_two_rel, last=False)
    sums = scatter_z(dot_back(hidden, wd[0]), dot_back(hidden, wd[1]))
    result = result_sum(scal, x_one, sums)
    d_w_gate = scatter_xy(
        scatter_core(dot_outer(rows_two[0], d_gate), dot_outer(rows_two[1], d_gate))
    )
    d_w_up = scatter_yx(scatter_core(dot_outer(rows_two[0], d_up), dot_outer(rows_two[1], d_up)))
    d_w_down = scatter_xy(
        scatter_core(dot_outer(rows_c[0], hidden), dot_outer(rows_c[1], hidden))
    ).T

    rows_m = gather_z(halves_of(dm))
    d_mix = dot_pair(rows_m, wo)
    d_pre_a, rl, qcum, end = mix_back(scal, d_mix, pre_a, h_ext, av)
    arrived = swap_channels(swap_send(end, 4))
    u_in = jnp.where(first_half, arrived, 0.0)
    d_w_out = scatter_yx(
        scatter_core(dot_outer(rows_m[0], mixer_in), dot_outer(rows_m[1], mixer_in))
    ).T
    d_w_a = scatter_xy(
        scatter_core(dot_outer(rows_one[0], d_pre_a), dot_outer(rows_one[1], d_pre_a))
    )
    d_pre_r, d_pre_i, d_pre_b, tail, head, sums8 = mix_grad(
        scal, rl, qcum, av, u_in, rate, inlet, conv, h_ext, ext, par, wr, wi
    )
    after = jnp.where(first_half, swap_channels(swap_send(head, 4)), 0.0)[:3]
    ahead = jnp.concatenate([jnp.zeros((16, WIDE), F32), after], axis=0)
    extra = par[0:1] * ahead[3:19]
    for k in range(1, 4):
        extra = extra + par[k : k + 1] * ahead[3 - k : 19 - k]
    tail = (tail + extra * par[ROW_MASK : ROW_MASK + 1]).astype(BF16)
    d_pre_b = lax.dynamic_update_slice_in_dim(d_pre_b, tail, (z ^ 3) * TOK + TOK - 16, 0)

    sums = scatter_z(
        dot_back(d_pre_a, wa[0]) + dot_back(d_pre_b, wb[0]),
        dot_back(d_pre_a, wa[1]) + dot_back(d_pre_b, wb[1]),
    )
    d_inputs, d_g_one = norm_back(scal, d_x_one, x_rel, sums, g_one_rel, last=True)
    d_w_b = scatter_yx(
        scatter_core(dot_outer(rows_one[0], d_pre_b), dot_outer(rows_one[1], d_pre_b))
    )

    def gate_grads(grads, c):
        full = dot_outer(xg[:, c * CH : (c + 1) * CH], grads[:, c * CH : (c + 1) * CH])
        return jnp.stack([full[:192, :192], full[192:, 192:]])

    def both(c):
        return jnp.stack([gate_grads(d_pre_r, c), gate_grads(d_pre_i, c)]).astype(BF16)

    def small_sum(own, other, dtype):
        a, c = swap_send(other, 4).astype(F32), swap_send(other, 68).astype(F32)
        b = swap_send(own, 64).astype(F32)
        total = ((own.astype(F32) + b) + (a + c)).astype(dtype)
        total = all_sum(total, Y_MASKS).astype(dtype)
        return total.astype(F32) + swap_send(total, CORE).astype(F32)

    d_gates = small_sum(both(0), both(1), BF16)
    sums8 = small_sum(sums8[:, :CH], sums8[:, CH:], F32)
    gains = jnp.concatenate([d_g_one, d_g_two], axis=0)
    gains = all_sum(gains, X_MASKS)
    gains = all_sum(gains, Y_MASKS)
    gains = gains + swap_send(gains, CORE)
    gains = all_sum(gains, Z_MASKS)

    in_second = (length > HALF_SEQ).astype(jnp.int32)
    window = lax.dynamic_slice_in_dim(ext, 5 + jnp.clip(length - HALF_SEQ * x_lo, 0, HALF_SEQ), 3, 0)
    window = jnp.where(x_lo == in_second, window, 0.0)
    state = jnp.where(first_half, 0.0, final[:1])
    ends = jnp.concatenate([window, state], axis=0)
    ends = ends[:, :CH] + swap_send(ends[:, CH:], 4)

    return (
        result[None],
        ends[3:4],
        ends[None, :3],
        d_inputs[None],
        gains[0],
        d_w_a,
        d_w_b,
        sums8[0:4],
        sums8[4],
        d_gates[0],
        d_gates[1],
        sums8[5],
        sums8[6],
        sums8[7],
        d_w_out,
        gains[1],
        d_w_gate,
        d_w_up,
        d_w_down,
    )


def solution(mesh):
    return jax.shard_map(
        on_device,
        mesh=mesh,
        in_specs=(
            P("dp", "mp", None),
            P("dp"),
            P("mp"),
            P("dp", "mp"),
            P("dp", None, "mp"),
            P(),
            P("dp", "mp"),
            P("dp", "mp"),
            P(None, "mp"),
            P("mp"),
            P("mp", None, None),
            P("mp", None, None),
            P("mp"),
            P("mp"),
            P("mp"),
            P("mp", "dp"),
            P(),
            P("dp", "mp"),
            P("dp", "mp"),
            P("mp", "dp"),
            P("dp", "mp", None),
        ),
        out_specs=(
            P("dp", "mp", None),
            P("dp", "mp"),
            P("dp", None, "mp"),
            P("dp", "mp", None),
            P(),
            P("dp", "mp"),
            P("dp", "mp"),
            P(None, "mp"),
            P("mp"),
            P("mp", None, None),
            P("mp", None, None),
            P("mp"),
            P("mp"),
            P("mp"),
            P("mp", "dp"),
            P(),
            P("dp", "mp"),
            P("dp", "mp"),
            P("mp", "dp"),
        ),
        check_vma=False,
    )
```

```python
import functools

import jax
import jax.numpy as jnp
from jax import lax
from jax.experimental import pallas as pl
from jax.experimental.pallas import tpu as pltpu
from jax.sharding import PartitionSpec as P

EPS = 1e-06
F32 = jnp.float32
BF16 = jnp.bfloat16
AXES = ("dp", "mp")
DEVICES = 128

Z_MASKS = (0, 1, 2, 3)
X_MASKS = (0, 4, 64, 68)
Y_MASKS = (0, 16, 32, 48)
CORE = 8
HALF_SEQ = 512
TOK = 128
CH = 384
WIDE = 768
CHUNKS = 8
STEPS = 64
GELU_A = 0.7978845608028654
GELU_B = 0.044715


def swap_send(values, mask):
    return lax.ppermute(values, AXES, [(i, i ^ mask) for i in range(DEVICES)])


def block_of(position, dp):
    mirrored = (position & 6) | ((position & 1) << 3) | ((position >> 3) & 1)
    return dp ^ mirrored


def gelu_parts(v):
    inner = GELU_A * (v + GELU_B * v * v * v)
    t = jnp.tanh(inner)
    half = 0.5 * (1.0 + t)
    slope = half + 0.5 * v * (1.0 - t * t) * (GELU_A * (1.0 + (3.0 * GELU_B) * v * v))
    return v * half, slope


def gelu_value(v):
    return v * (0.5 * (1.0 + jnp.tanh(GELU_A * (v + GELU_B * v * v * v))))


def neg_expm1(v):
    series = 1.0 + v * (1.0 / 9.0)
    for n in range(8, 1, -1):
        series = 1.0 + (v * (1.0 / n)) * series
    return jnp.where(v > -0.5, -v * series, 1.0 - jnp.exp(v))


def vmem(limit):
    return pltpu.CompilerParams(vmem_limit_bytes=limit * 1024 * 1024)


SMEM_SPEC = pl.BlockSpec(memory_space=pltpu.SMEM)


def block_rows(dp, p):
    return pl.ds(pl.multiple_of(block_of(p, dp) * 128, 128), 128)


def cols(p):
    return slice(p * 128, (p + 1) * 128)


def prep_kernel(scal, x_ref, g_ref, n_ref):
    dp = scal[2]
    x = x_ref[...].astype(F32)
    s = lax.rsqrt(jnp.mean(x * x, axis=-1, keepdims=True) + EPS)
    for p in range(16):
        src = block_rows(dp, p)
        n_ref[:, cols(p)] = (x_ref[:, src].astype(F32) * s * g_ref[:, src]).astype(BF16)


def prep(scal, x, g):
    return pl.pallas_call(
        prep_kernel,
        out_shape=jax.ShapeDtypeStruct((TOK, 2048), BF16),
        in_specs=[SMEM_SPEC] + [pl.BlockSpec(memory_space=pltpu.VMEM)] * 2,
        compiler_params=vmem(16),
        name="prep",
    )(scal, x, g)


def to_relative_kernel(scal, rows_ref, out0, out1):
    for p in range(16):
        out = (out0, out1)[p // 8]
        out[:, cols(p % 8)] = rows_ref[:, block_rows(scal[2], p)]


def to_relative(scal, rows):
    n = rows.shape[0]
    return pl.pallas_call(
        to_relative_kernel,
        grid=(2,),
        out_shape=(jax.ShapeDtypeStruct((n, 1024), rows.dtype),) * 2,
        in_specs=[SMEM_SPEC, pl.BlockSpec((n // 2, 2048), lambda i: (i, 0))],
        out_specs=(pl.BlockSpec((n // 2, 1024), lambda i: (i, 0)),) * 2,
        compiler_params=vmem(16),
        name="to_relative",
    )(scal, rows)


def gain_kernel(scal, in0, in1, out):
    for p in range(16):
        out[:, block_rows(scal[2], p)] = (in0, in1)[p // 8][:, cols(p % 8)]


def from_relative_gain(scal, g0, g1):
    return pl.pallas_call(
        gain_kernel,
        out_shape=jax.ShapeDtypeStruct((1, 2048), F32),
        in_specs=[SMEM_SPEC] + [pl.BlockSpec(memory_space=pltpu.VMEM)] * 2,
        name="gain_order",
    )(scal, g0, g1)


def assemble_kernel(scal, own, p1, p2_0, p2_1, p3, *outs):
    z = scal[0]
    for j, block in enumerate((own, p1, None, p3)):
        rows = pl.ds(pl.multiple_of((z ^ j) * TOK, TOK), TOK)
        for h in (0, 1):
            part = slice(h * 1024, (h + 1) * 1024)
            value = (p2_0, p2_1)[h][...] if block is None else block[:, part]
            if len(outs) == 2:
                outs[h][rows, :] = value
            else:
                outs[0][rows, part] = value


def assemble(scal, blocks, halves):
    shape = jax.ShapeDtypeStruct((HALF_SEQ, 1024 if halves else 2048), BF16)
    return pl.pallas_call(
        assemble_kernel,
        out_shape=(shape, shape) if halves else shape,
        in_specs=[SMEM_SPEC] + [pl.BlockSpec(memory_space=pltpu.VMEM)] * 5,
        compiler_params=vmem(16),
        name="assemble",
    )(scal, *blocks)


def add_blocks(dp, sums, base, out):
    own0, own1, a, b = sums
    for p in range(16):
        own = (own0, own1)[p // 8][:, cols(p % 8)]
        dst = block_rows(dp, p)
        total = own + a[:, cols(p)].astype(F32) + b[:, cols(p)].astype(F32)
        out[:, dst] = total if base is None else base[:, dst].astype(F32) + total


def mid_kernel(scal, x_ref, own0, own1, a, b, g_ref, xo_ref, n_ref):
    add_blocks(scal[2], (own0, own1, a, b), x_ref, xo_ref)
    x = xo_ref[...]
    s = lax.rsqrt(jnp.mean(x * x, axis=-1, keepdims=True) + EPS)
    n_ref[...] = (x * s * g_ref[...]).astype(BF16)


def mid_norm(scal, x, sums, g):
    return pl.pallas_call(
        mid_kernel,
        out_shape=(
            jax.ShapeDtypeStruct((TOK, 2048), F32),
            jax.ShapeDtypeStruct((TOK, 2048), BF16),
        ),
        in_specs=[SMEM_SPEC] + [pl.BlockSpec(memory_space=pltpu.VMEM)] * 6,
        compiler_params=vmem(16),
        name="mid_norm",
    )(scal, x, *sums, g)


def norm_gradient(x, g, dn):
    s = lax.rsqrt(jnp.mean(x * x, axis=-1, keepdims=True) + EPS)
    w = g * dn
    inner = jnp.mean(w * x, axis=-1, keepdims=True)
    return s * (w - x * (s * s * inner)), s


def back_two_kernel(scal, c_ref, x_ref, own0, own1, a, b, g_ref, dx_ref, dm_ref, dg_ref):
    own = jnp.concatenate([own0[...], own1[...]], axis=1)
    dn = own + a[...].astype(F32) + b[...].astype(F32)
    x = x_ref[...]
    back, s = norm_gradient(x, g_ref[...], dn)
    dg_ref[...] = jnp.sum(dn * x * s, axis=0, keepdims=True)
    dx_ref[...] = c_ref[...].astype(F32) + back
    for p in range(16):
        dm_ref[:, cols(p)] = dx_ref[:, block_rows(scal[2], p)].astype(BF16)


def norm_back_two(scal, c, x, sums, g):
    return pl.pallas_call(
        back_two_kernel,
        out_shape=(
            jax.ShapeDtypeStruct((TOK, 2048), F32),
            jax.ShapeDtypeStruct((TOK, 2048), BF16),
            jax.ShapeDtypeStruct((1, 2048), F32),
        ),
        in_specs=[SMEM_SPEC] + [pl.BlockSpec(memory_space=pltpu.VMEM)] * 7,
        compiler_params=vmem(24),
        name="norm_back_two",
    )(scal, c, x, *sums, g)


def back_one_kernel(scal, base_ref, x_ref, own0, own1, a, b, g_ref, dx_ref, dn_ref):
    add_blocks(scal[2], (own0, own1, a, b), None, dn_ref)
    back, _ = norm_gradient(x_ref[...].astype(F32), g_ref[...], dn_ref[...])
    dx_ref[...] = base_ref[...] + back


def norm_back_one(scal, base, x, sums, g):
    return pl.pallas_call(
        back_one_kernel,
        out_shape=jax.ShapeDtypeStruct((TOK, 2048), F32),
        in_specs=[SMEM_SPEC] + [pl.BlockSpec(memory_space=pltpu.VMEM)] * 7,
        scratch_shapes=[pltpu.VMEM((TOK, 2048), F32)],
        compiler_params=vmem(24),
        name="norm_back_one",
    )(scal, base, x, *sums, g)


PACK_ROWS = 16
ROW_CB, ROW_BR, ROW_BI, ROW_DECAY, ROW_MASK, ROW_H, ROW_SIG = 4, 5, 6, 7, 8, 9, 10


def row(ref, i):
    return ref[i : i + 1, :]


def valid_rows(scal, start, size):
    t = lax.broadcasted_iota(jnp.int32, (size, 1), 0) + (scal[1] * HALF_SEQ + start)
    return t < scal[3]


GROUPS = 3


def pack_kernel(sizes, cw, cb, br, bi, lam, h, cs, out):
    slot = lax.broadcasted_iota(jnp.int32, (1, CH), 1)
    limit = jnp.where(slot < 192, sizes[0], 192 + sizes[1])
    mask = jnp.where(slot < limit, 1.0, 0.0)
    out[...] = jnp.zeros_like(out)
    out[0:4, :] = cw[...]
    out[ROW_CB : ROW_CB + 1, :] = cb[...]
    out[ROW_BR : ROW_BR + 1, :] = br[...]
    out[ROW_BI : ROW_BI + 1, :] = bi[...]
    out[ROW_DECAY : ROW_DECAY + 1, :] = -8.0 * jax.nn.softplus(-lam[...])
    out[ROW_MASK : ROW_MASK + 1, :] = mask
    out[ROW_H : ROW_H + 1, :] = h[...] * mask
    out[ROW_SIG : ROW_SIG + 1, :] = jax.nn.sigmoid(-lam[...])
    out[11:14, :] = cs[...] * mask


def make_pack(head_sizes, *rows):
    return pl.pallas_call(
        pack_kernel,
        out_shape=jax.ShapeDtypeStruct((PACK_ROWS, CH), F32),
        in_specs=[SMEM_SPEC] + [pl.BlockSpec(memory_space=pltpu.VMEM)] * 7,
        name="pack",
    )(head_sizes, *rows)


def put(ref, rows, value):
    for g in range(GROUPS):
        ref[g, rows, :] = value[:, g * 128 : (g + 1) * 128]


def take(ref, rows):
    return jnp.concatenate([ref[g, rows, :] for g in range(GROUPS)], axis=1)


def at_step(ref, s):
    rows = pl.ds(s, CHUNKS, stride=STEPS)
    return [ref.at[g][rows, :] for g in range(GROUPS)]


def put_step(ref, s, values):
    rows = pl.ds(s, CHUNKS, stride=STEPS)
    for g in range(GROUPS):
        ref.at[g][rows, :] = values[g]


def run_steps(step):
    start = [jnp.zeros((CHUNKS, 128), F32)] * GROUPS + [jnp.ones((CHUNKS, 128), F32)] * GROUPS
    out = lax.fori_loop(0, STEPS, step, tuple(start), unroll=4)
    return jnp.concatenate(out[:GROUPS], axis=1), jnp.concatenate(out[GROUPS:], axis=1)


def mix_fwd_kernel(
    scal, pre_b, halo, par, wr, wi, rate, inlet, conv, xg, av, hl, pcum, ext, end, bv
):
    mask = row(par, ROW_MASK)
    ext[0:8, :] = halo[...]
    for c in range(CHUNKS):
        ext[8 + c * STEPS : 8 + (c + 1) * STEPS, :] = pre_b[c * STEPS : (c + 1) * STEPS, :] * mask
    for c in range(CHUNKS):
        t0 = c * STEPS
        acc = row(par, ROW_CB) + row(par, 0) * ext[t0 + 5 : t0 + 5 + STEPS, :]
        for k in range(1, 4):
            acc = acc + row(par, k) * ext[t0 + 5 + k : t0 + 5 + k + STEPS, :]
        acc = acc * mask
        conv[t0 : t0 + STEPS, :] = acc
        xg[t0 : t0 + STEPS, :] = acc.astype(BF16)
    rate[...] = jnp.dot(xg[...], wr[0], preferred_element_type=F32)
    inlet[...] = jnp.dot(xg[...], wi[0], preferred_element_type=F32)
    for c in range(CHUNKS):
        rows = slice(c * STEPS, (c + 1) * STEPS)
        r = jax.nn.sigmoid(rate[rows, :] + row(par, ROW_BR))
        i = jax.nn.sigmoid(inlet[rows, :] + row(par, ROW_BI))
        rate[rows, :] = r
        inlet[rows, :] = i
        log_a = row(par, ROW_DECAY) * r
        mult = jnp.sqrt(neg_expm1(2.0 * log_a))
        valid = valid_rows(scal, c * STEPS, STEPS)
        put(av, rows, jnp.where(valid, jnp.exp(log_a), 1.0))
        put(bv, rows, jnp.where(valid, mult * i * conv[rows, :], 0.0))

    def step(s, carry):
        a, b = at_step(av, s), at_step(bv, s)
        h = [a[g] * carry[g] + b[g] for g in range(GROUPS)]
        p = [a[g] * carry[GROUPS + g] for g in range(GROUPS)]
        put_step(hl, s, h)
        put_step(pcum, s, p)
        return tuple(h + p)

    h, p = run_steps(step)
    carry = row(par, ROW_H)
    for c in range(CHUNKS):
        carry = h[c : c + 1, :] + p[c : c + 1, :] * carry
    end[...] = jnp.broadcast_to(carry, (8, CH))


def wide(rows):
    return pl.BlockSpec((rows, CH), lambda i: (0, i))


GATE_SPEC = pl.BlockSpec((1, CH, CH), lambda i: (i, 0, 0))


STRIP_SPEC = pl.BlockSpec((GROUPS, 512, 128), lambda i: (i, 0, 0))
STRIP = jax.ShapeDtypeStruct((2 * GROUPS, 512, 128), F32)
STRIP_SCRATCH = pltpu.VMEM((GROUPS, 512, 128), F32)


def sds(rows, dtype=F32):
    return jax.ShapeDtypeStruct((rows, WIDE), dtype)


def mix_fwd(scal, pre_b, halo, par, wr, wi):
    return pl.pallas_call(
        mix_fwd_kernel,
        grid=(2,),
        out_shape=(
            sds(512), sds(512), sds(512), sds(512, BF16), STRIP, STRIP, STRIP, sds(520), sds(8),
        ),
        in_specs=[SMEM_SPEC, wide(512), wide(8), wide(16), GATE_SPEC, GATE_SPEC],
        out_specs=(
            wide(512), wide(512), wide(512), wide(512), STRIP_SPEC, STRIP_SPEC, STRIP_SPEC, wide(520), wide(8),
        ),
        scratch_shapes=[STRIP_SCRATCH],
        compiler_params=vmem(32),
        name="mix_fwd",
    )(scal, pre_b, halo, par, wr, wi)


def mix_out_kernel(scal, hl, pcum, pre_a, h_in, h_ext, mixed, final):
    h_ext[0:8, :] = h_in[...]
    carry = row(h_in, 7)
    for c in range(CHUNKS):
        rows = slice(c * STEPS, (c + 1) * STEPS)
        h = take(hl, rows) + take(pcum, rows) * carry
        h_ext[8 + c * STEPS : 8 + (c + 1) * STEPS, :] = h
        carry = h[STEPS - 1 : STEPS, :]
        mixed[rows, :] = (gelu_value(pre_a[rows, :]) * h).astype(BF16)
    final[...] = jnp.broadcast_to(carry, (8, CH))


def mix_out(scal, hl, pcum, pre_a, h_in):
    return pl.pallas_call(
        mix_out_kernel,
        grid=(2,),
        out_shape=(sds(520), sds(512, BF16), sds(8)),
        in_specs=[SMEM_SPEC, STRIP_SPEC, STRIP_SPEC, wide(512), wide(8)],
        out_specs=(wide(520), wide(512), wide(8)),
        compiler_params=vmem(32),
        name="mix_out",
    )(scal, hl, pcum, pre_a, h_in)


def mix_back_kernel(scal, d_mix, pre_a, h_ext, av, d_pre_a, rl, qcum, end, dh):
    for c in range(CHUNKS):
        rows = slice(c * STEPS, (c + 1) * STEPS)
        act, slope = gelu_parts(pre_a[rows, :])
        dm = d_mix[rows, :]
        h = h_ext[8 + c * STEPS : 8 + (c + 1) * STEPS, :]
        d_pre_a[rows, :] = (slope * h * dm).astype(BF16)
        put(dh, rows, dm * act)

    def step(n, carry):
        s = STEPS - 1 - n
        a, d = at_step(av, s), at_step(dh, s)
        carried = [d[g] + carry[g] for g in range(GROUPS)]
        put_step(rl, s, carried)
        put_step(qcum, s, carry[GROUPS:])
        u = [a[g] * carried[g] for g in range(GROUPS)]
        return tuple(u + [a[g] * carry[GROUPS + g] for g in range(GROUPS)])

    u, q = run_steps(step)
    carry = jnp.zeros((1, CH), F32)
    for c in range(CHUNKS - 1, -1, -1):
        carry = u[c : c + 1, :] + q[c : c + 1, :] * carry
    end[...] = jnp.broadcast_to(carry, (8, CH))


def mix_back(scal, d_mix, pre_a, h_ext, av):
    return pl.pallas_call(
        mix_back_kernel,
        grid=(2,),
        out_shape=(sds(512, BF16), STRIP, STRIP, sds(8)),
        in_specs=[SMEM_SPEC, wide(512), wide(512), wide(520), STRIP_SPEC],
        out_specs=(wide(512), STRIP_SPEC, STRIP_SPEC, wide(8)),
        scratch_shapes=[STRIP_SCRATCH],
        compiler_params=vmem(32),
        name="mix_back",
    )(scal, d_mix, pre_a, h_ext, av)


def total_rows(v):
    return jnp.sum(v, axis=0, keepdims=True)


def mix_grad_kernel(
    scal, rl, qcum, av, u_in, rate, inlet, conv, h_ext, ext, par, wr, wi,
    d_pre_r, d_pre_i, d_pre_b, tail, head, sums, dconv,
):
    mask = row(par, ROW_MASK)
    carry = row(u_in, 0)
    d_lam = jnp.zeros((1, CH), F32)
    d_br = jnp.zeros((1, CH), F32)
    d_bi = jnp.zeros((1, CH), F32)
    for c in range(CHUNKS - 1, -1, -1):
        t0 = c * STEPS
        rows = slice(t0, t0 + STEPS)
        a = take(av, rows)
        carried = take(rl, rows) + take(qcum, rows) * carry
        carry = a[0:1, :] * carried[0:1, :]
        valid = valid_rows(scal, t0, STEPS)
        d_drive = jnp.where(valid, carried, 0.0)
        d_decay = d_drive * h_ext[t0 + 7 : t0 + 7 + STEPS, :]
        r, i, x = rate[rows, :], inlet[rows, :], conv[rows, :]
        gap = neg_expm1(2.0 * (row(par, ROW_DECAY) * r))
        inv = lax.rsqrt(gap)
        mult = gap * inv
        driven = d_drive * i
        d_log = d_decay * a - driven * x * (a * a) * inv
        d_lam = d_lam + total_rows(d_log * r)
        pr = (d_log * row(par, ROW_DECAY) * r * (1.0 - r)).astype(BF16)
        pi = (d_drive * mult * x * i * (1.0 - i)).astype(BF16)
        d_pre_r[rows, :] = pr
        d_pre_i[rows, :] = pi
        d_br = d_br + total_rows(pr.astype(F32))
        d_bi = d_bi + total_rows(pi.astype(F32))
        dconv[rows, :] = driven * mult
    dims = (((1,), (1,)), ((), ()))
    gate = lax.dot_general(d_pre_r[...], wr[0], dims, preferred_element_type=F32)
    gate = gate + lax.dot_general(d_pre_i[...], wi[0], dims, preferred_element_type=F32)
    dconv[0:HALF_SEQ, :] = (dconv[0:HALF_SEQ, :] + gate) * mask
    dconv[HALF_SEQ : HALF_SEQ + 8, :] = jnp.zeros((8, CH), F32)
    head[...] = dconv[0:8, :]
    taps = [jnp.zeros((1, CH), F32) for _ in range(4)]
    bias = jnp.zeros((1, CH), F32)
    for c in range(CHUNKS):
        t0 = c * STEPS
        here = dconv[t0 : t0 + STEPS, :]
        bias = bias + total_rows(here)
        back = jnp.zeros((STEPS, CH), F32)
        for k in range(4):
            taps[k] = taps[k] + total_rows(here * ext[t0 + 5 + k : t0 + 5 + k + STEPS, :])
            back = back + row(par, k) * dconv[t0 + 3 - k : t0 + 3 - k + STEPS, :]
        back = back * mask
        d_pre_b[t0 : t0 + STEPS, :] = back.astype(BF16)
        if c == CHUNKS - 1:
            tail[...] = back[STEPS - 16 :, :]
    for k in range(4):
        sums[k : k + 1, :] = taps[k]
    sums[4:5, :] = bias
    sums[5:6, :] = d_br
    sums[6:7, :] = d_bi
    sums[7:8, :] = 8.0 * row(par, ROW_SIG) * d_lam


def mix_grad(scal, rl, qcum, av, u_in, rate, inlet, conv, h_ext, ext, par, wr, wi):
    return pl.pallas_call(
        mix_grad_kernel,
        grid=(2,),
        out_shape=(sds(512, BF16), sds(512, BF16), sds(512, BF16), sds(16), sds(8), sds(8)),
        in_specs=[
            SMEM_SPEC, STRIP_SPEC, STRIP_SPEC, STRIP_SPEC, wide(8), wide(512), wide(512), wide(512),
            wide(520), wide(520), wide(16), GATE_SPEC, GATE_SPEC,
        ],
        out_specs=(wide(512), wide(512), wide(512), wide(16), wide(8), wide(8)),
        scratch_shapes=[pltpu.VMEM((HALF_SEQ + 8, CH), F32)],
        compiler_params=vmem(40),
        name="mix_grad",
    )(scal, rl, qcum, av, u_in, rate, inlet, conv, h_ext, ext, par, wr, wi)


def tie(values, *earlier):
    return lax.optimization_barrier((values, earlier))[0]


def gather_z(own):
    p1 = swap_send(own, 1)
    p3 = swap_send(own, 3)
    p2_0 = swap_send(p3[:, :1024], 1)
    p2_1 = swap_send(p1[:, 1024:], 3)
    return own, p1, p2_0, p2_1, p3


def scatter_z(z, part0, part1):
    def block(part, j):
        return lax.dynamic_slice_in_dim(part, (z ^ j) * TOK, TOK, 0)

    far_0 = swap_send(block(part0, 2).astype(BF16), 1)
    far_1 = swap_send(block(part1, 2).astype(BF16), 3)
    to_1 = [block(part0, 1).astype(BF16), (block(part1, 1) + far_1.astype(F32)).astype(BF16)]
    to_3 = [(block(part0, 3) + far_0.astype(F32)).astype(BF16), block(part1, 3).astype(BF16)]
    r1 = swap_send(jnp.concatenate(to_1, axis=1), 1)
    r3 = swap_send(jnp.concatenate(to_3, axis=1), 3)
    return block(part0, 0), block(part1, 0), r1, r3


Z_GROUPS = [[0, 1, 2, 3], [4, 5, 6, 7]]


def reduce_z(values):
    return lax.psum_scatter(
        values, "mp", scatter_dimension=0, axis_index_groups=Z_GROUPS, tiled=True
    )


def cross(axis, blocks):
    return jnp.concatenate(
        [
            jnp.concatenate([blocks[0], blocks[1]], axis=-1),
            jnp.concatenate([blocks[2], blocks[3]], axis=-1),
        ],
        axis=axis,
    )


def join_mixer_kernel(*refs):
    one, two, out = refs[:4], refs[4:8], refs[8]
    for y in range(4):
        rows = slice(y * 256, (y + 1) * 256)
        out[rows, :CH] = one[y][:, :CH]
        out[rows, CH:WIDE] = one[y][:, 512 : 512 + CH]
        out[rows, 2 * WIDE : 2 * WIDE + 128] = one[y][:, CH:512]
        out[rows, 2 * WIDE + CH : 2 * WIDE + CH + 128] = one[y][:, 512 + CH :]
        for r in (0, 1):
            rows = slice(y * 256 + r * 128, y * 256 + (r + 1) * 128)
            own, other = two[2 * r], two[2 * r + 1]
            out[rows, WIDE : WIDE + CH] = own[y, :, :CH]
            out[rows, WIDE + CH : 2 * WIDE] = other[y, :, :CH]
            out[rows, 2 * WIDE + 128 : 2 * WIDE + CH] = own[y, :, CH:]
            out[rows, 2 * WIDE + CH + 128 :] = other[y, :, CH:]


def join_mixer(one, two):
    return pl.pallas_call(
        join_mixer_kernel,
        out_shape=jax.ShapeDtypeStruct((1024, 3 * WIDE), BF16),
        compiler_params=vmem(24),
        name="join_mixer",
    )(*one, *two)


def sum_four(own, a, b, c):
    return (own.astype(F32) + a.astype(F32)) + (b.astype(F32) + c.astype(F32))


def add_low(a, b):
    return (a.astype(F32) + b.astype(F32)).astype(BF16)


def y_pieces(total):
    return [total[k * 256 : (k + 1) * 256] for k in range(4)]


def x_pieces(total):
    n = total.shape[-1] // 2
    return [total[:, r * 128 : (r + 1) * 128, c * n : (c + 1) * n] for r in (0, 1) for c in (0, 1)]


def send_three(pieces, masks):
    return [swap_send(v, m) for v, m in zip(pieces[1:], masks[1:])]


def first_y(total):
    py = y_pieces(total)
    received = send_three(py, Y_MASKS)
    pieces = [v[0] for v in x_pieces(sum_four(py[0], *received).astype(BF16)[None])]
    return received, pieces, X_MASKS


def first_x(total):
    px = x_pieces(total.reshape(4, 256, -1))
    received = send_three(px, X_MASKS)
    total = sum_four(px[0], *received).astype(BF16)
    return received, [total[k] for k in range(4)], Y_MASKS


def finish_kernel(*refs, turned):
    total = sum_four(*[r[...] for r in refs[:4]])
    at = 0
    for out, turn in zip(refs[4:], turned):
        n = out.shape[0] if turn else out.shape[1]
        part = total[:, at : at + n]
        out[...] = part.T if turn else part
        at += n


def finish(stage, *turned):
    _, pieces, masks = stage
    terms = [pieces[0]] + send_three(pieces, masks)
    n = pieces[0].shape[1] // len(turned)
    shapes = [jax.ShapeDtypeStruct((n, TOK) if t else (TOK, n), F32) for t in turned]
    return pl.pallas_call(
        functools.partial(finish_kernel, turned=turned),
        out_shape=tuple(shapes),
        compiler_params=vmem(16),
        name="finish",
    )(*terms)


def outer_mlp_kernel(n_ref, c_ref, gu_ref, h_ref, out_ref, turned):
    step = pl.program_id(0)

    @pl.when(step == 0)
    def _():
        turned[...] = n_ref[...].T

    @pl.when(step == 6)
    def _():
        turned[...] = c_ref[...].T

    @pl.when(step < 6)
    def _():
        out_ref[...] = jnp.dot(turned[...], gu_ref[...], preferred_element_type=F32).astype(BF16)

    @pl.when(step >= 6)
    def _():
        out_ref[...] = jnp.dot(turned[...], h_ref[...], preferred_element_type=F32).astype(BF16)


def outer_mlp(rows_two, rows_c, d_gate_up, hidden):
    whole = pl.BlockSpec((HALF_SEQ, 2048), lambda i: (0, 0))
    return pl.pallas_call(
        outer_mlp_kernel,
        grid=(9,),
        out_shape=jax.ShapeDtypeStruct((2048, 6 * WIDE), BF16),
        in_specs=[
            whole,
            whole,
            pl.BlockSpec((HALF_SEQ, 512), lambda i: (0, jnp.minimum(i, 5))),
            pl.BlockSpec((HALF_SEQ, 512), lambda i: (0, jnp.maximum(i - 6, 0))),
        ],
        out_specs=pl.BlockSpec((2048, 512), lambda i: (0, i)),
        scratch_shapes=[pltpu.VMEM((2048, HALF_SEQ), BF16)],
        compiler_params=vmem(40),
        cost_estimate=pl.CostEstimate(
            flops=2 * 2048 * 4608 * 512, bytes_accessed=30 * 2**20, transcendentals=0
        ),
        name="outer_mlp",
    )(rows_two, rows_c, d_gate_up, hidden)


def finish_mlp_kernel(mine, other, gate, up, down):
    for k, out in enumerate((gate, up)):
        own = mine[:, 2 * k * WIDE : (2 * k + 1) * WIDE]
        out[...] = own.astype(F32) + other[:, k * WIDE : (k + 1) * WIDE].astype(F32)
    own = mine[:, 4 * WIDE : 5 * WIDE]
    down[...] = (own.astype(F32) + other[:, 2 * WIDE :].astype(F32)).T


def finish_mlp(shards):
    given = jnp.concatenate(
        [shards[:, k * WIDE : (k + 1) * WIDE] for k in (1, 3, 5)], axis=1
    )
    shape = jax.ShapeDtypeStruct((TOK, WIDE), F32)
    return pl.pallas_call(
        finish_mlp_kernel,
        out_shape=(shape, shape, jax.ShapeDtypeStruct((WIDE, TOK), F32)),
        compiler_params=vmem(16),
        name="finish_mlp",
    )(shards, swap_send(given, 4))


def swap_channels(v):
    return jnp.concatenate([v[..., CH:], v[..., :CH]], axis=-1)


def dot(a, b):
    return jnp.dot(a, b, preferred_element_type=F32)


def dot_back(a, b):
    return lax.dot_general(a, b, (((1,), (1,)), ((), ())), preferred_element_type=F32)


def dot_outer(a, b):
    return lax.dot_general(a, b, (((0,), (0,)), ((), ())), preferred_element_type=F32)


def pair_blocks(w):
    zero = jnp.zeros_like(w[..., 0, :, :])
    top = jnp.concatenate([w[..., 0, :, :], zero], axis=-1)
    low_rows = jnp.concatenate([zero, w[..., 1, :, :]], axis=-1)
    return jnp.concatenate([top, low_rows], axis=-2)


def on_device(
    inputs,
    lengths,
    head_sizes,
    h_start,
    conv_start,
    g_one,
    w_a,
    w_b,
    conv_w,
    conv_b,
    w_r,
    w_i,
    b_r,
    b_i,
    lam,
    w_out,
    g_two,
    w_gate,
    w_up,
    w_down,
    cotangent,
):
    dp = lax.axis_index("dp").astype(jnp.int32)
    mp = lax.axis_index("mp").astype(jnp.int32)
    z, x_lo, core = mp % 4, mp // 4, dp % 2
    length = lengths[0]
    scal = jnp.stack([z, x_lo, dp, length])
    first_half = x_lo == 0
    g_one, g_two = g_one[None], g_two[None]

    shard = jnp.concatenate([w_gate, w_up, w_down.T], axis=1)

    out_t = w_out.T
    first = jnp.concatenate([w_a, out_t[:, :128]], axis=1)
    second = jnp.concatenate([w_b, out_t[:, 128:]], axis=1)
    gates = jnp.stack([w_r, w_i])
    pair = swap_send(jnp.concatenate([first, shard, gates.reshape(TOK, 1152)], axis=1), 4)
    y1, y3 = swap_send(second, 16), swap_send(second, 48)
    x3 = swap_send(first, 68)
    x = inputs[0]
    c = cotangent[0]
    c1, c3 = swap_send(c, 1), swap_send(c, 3)
    pack = make_pack(
        head_sizes, conv_w, conv_b[None], b_r[None], b_i[None], lam[None], h_start, conv_start[0]
    )
    far_first, far_second, pack = tie((first, second, pack), y1, y3, x3)
    x2, y2 = swap_send(far_first, 64), swap_send(far_second, 32)
    pack_other = swap_send(pack, 4)
    n_one = tie(prep(scal, x, g_one), x2, y2, pack_other, c1, c3)
    z1, z3 = swap_send(n_one, 1), swap_send(n_one, 3)
    pair = tie(pair, x2, y2, c1, c3)
    x1, other, gates_other = pair[:, :512], pair[:, 512:2816], pair[:, 2816:]
    shard = jnp.concatenate(
        [v[:, i * WIDE : (i + 1) * WIDE] for i in range(3) for v in (shard, other)], axis=1
    )
    w_mlp = lax.all_gather(shard, "dp", axis=0, tiled=True)

    par = jnp.concatenate([pack, pack_other], axis=1)
    gates = pair_blocks(jnp.stack([gates, gates_other.reshape(gates.shape)], axis=1))
    wr, wi = gates[0], gates[1]
    rows = cross(0, [first, x1, x2, x3])
    stack = jnp.stack([second, y1, y2, y3], axis=0)
    rows, stack = tie((rows, stack), n_one)
    ry1, ry3, sx2 = swap_send(rows, 16), swap_send(rows, 48), swap_send(stack, 64)
    z2_0, z2_1 = swap_send(z3[:, :1024], 1), swap_send(z1[:, 1024:], 3)
    far_rows, far_stack = tie((rows, stack), ry1, ry3, sx2, z1, z3)
    ry2, sx1, sx3 = swap_send(far_rows, 32), swap_send(far_stack, 4), swap_send(far_stack, 68)
    ry2, sx1, sx3 = tie((ry2, sx1, sx3), z2_0, z2_1)
    mixer = join_mixer((rows, ry1, ry2, ry3), (stack, sx1, sx2, sx3))
    rows_one = assemble(scal, (n_one, z1, z2_0, z2_1, z3), True)
    mixers = (mixer, swap_send(mixer, CORE))
    wa = [m[:, :WIDE] for m in mixers]
    wb = [m[:, WIDE : 2 * WIDE] for m in mixers]
    wo = [m[:, 2 * WIDE :] for m in mixers]

    pre_b = dot(rows_one[0], wb[0]) + dot(rows_one[1], wb[1])
    edge = swap_channels(swap_send(pre_b[HALF_SEQ - 8 :], 4)) * par[ROW_MASK : ROW_MASK + 1]
    start_halo = jnp.concatenate([jnp.zeros((5, WIDE), F32), par[11:14]], axis=0)
    halo = jnp.where(first_half, start_halo, edge)
    par_used = par.at[ROW_H].set(jnp.where(first_half, par[ROW_H], 0.0))
    pre_a = dot(rows_one[0], wa[0]) + dot(rows_one[1], wa[1])
    rate, inlet, conv, xg, av, hl, pcum, ext, end = mix_fwd(scal, pre_b, halo, par_used, wr, wi)
    arrived = swap_channels(swap_send(end, 4))
    h_in = jnp.where(first_half, jnp.broadcast_to(par[ROW_H : ROW_H + 1], (8, WIDE)), arrived)
    c3_sent, c1_sent = tie((c3[:, :1024], c1[:, 1024:]), rows_one[0])
    c2_0, c2_1 = swap_send(c3_sent, 1), swap_send(c1_sent, 3)
    h_in = tie(h_in, c2_0, c2_1)
    h_ext, mixer_in, final = mix_out(scal, hl, pcum, pre_a, h_in)
    sums = scatter_z(z, dot_back(mixer_in, wo[0]), dot_back(mixer_in, wo[1]))
    rows_c = assemble(scal, (c, c1, c2_0, c2_1, c3), False)
    x_one, n_two = mid_norm(scal, x, sums, g_two)

    w_gate_up, w_dn = w_mlp[:, : 4 * WIDE], w_mlp[:, 4 * WIDE :]
    rows_two = assemble(scal, gather_z(n_two), False)
    gate_up = dot(rows_two, w_gate_up)
    d_hidden = dot(rows_c, w_dn)
    gate_pre, up_pre = gate_up[:, : 2 * WIDE], gate_up[:, 2 * WIDE :]
    act, slope = gelu_parts(gate_pre)
    hidden = (act * up_pre).astype(BF16)
    d_gate = (slope * (up_pre * d_hidden)).astype(BF16)
    d_up = (act * d_hidden).astype(BF16)
    d_gate_up = jnp.concatenate([d_gate, d_up], axis=1)
    d_rows = dot_back(d_gate_up, w_gate_up)
    d_w_mlp = outer_mlp(rows_two, rows_c, tie(d_gate_up, d_rows), hidden)
    shards = lax.psum_scatter(d_w_mlp, "dp", scatter_dimension=0, tiled=True)
    sums = scatter_z(z, d_rows[:, :1024], d_rows[:, 1024:])
    d_x_one, dm, d_g_two = norm_back_two(scal, c, x_one, sums, g_two)

    def outer_core(rows, grads):
        given, mine = [dot_outer(rows[h], grads).astype(BF16) for h in (1, 0)]
        return mine, swap_send(given, CORE)

    d_result = dot_back(tie(hidden, d_w_mlp), w_dn).astype(BF16)
    dm = tie(dm, d_result)

    rows_m = list(assemble(scal, gather_z(dm), True))
    d_mix = dot(rows_m[0], wo[0]) + dot(rows_m[1], wo[1])
    d_pre_a, rl, qcum, end = mix_back(scal, d_mix, pre_a, h_ext, av)
    arrived = swap_channels(swap_send(end, 4))
    u_in = jnp.where(first_half, arrived, 0.0)

    def own_first(o, a):
        return jnp.concatenate([o[:, :CH], a[:, :CH], o[:, CH:], a[:, CH:]], axis=1)

    oa = [
        own_first(
            dot_outer(rows_m[h], mixer_in).astype(BF16), dot_outer(rows_one[h], d_pre_a).astype(BF16)
        )
        for h in (0, 1)
    ]
    oa[1] = swap_send(oa[1], CORE)
    u_in = tie(u_in, oa[1])
    oa = first_y(add_low(*oa))
    d_w_out, d_w_a = finish(oa, True, False)
    d_pre_r, d_pre_i, d_pre_b, tail, head, sums8 = mix_grad(
        scal, rl, qcum, av, u_in, rate, inlet, conv, h_ext, ext, par, wr, wi
    )
    d_result = reduce_z(tie(d_result, head))
    result = (x_one + d_result.astype(F32)).astype(BF16)
    after = jnp.where(first_half, swap_channels(swap_send(head, 4)), 0.0)[:3]
    ahead = jnp.concatenate([jnp.zeros((16, WIDE), F32), after], axis=0)
    extra = par[0:1] * ahead[3:19]
    for k in range(1, 4):
        extra = extra + par[k : k + 1] * ahead[3 - k : 19 - k]
    tail = (tail + extra * par[ROW_MASK : ROW_MASK + 1]).astype(BF16)
    d_pre_b = lax.dynamic_update_slice_in_dim(d_pre_b, tail, HALF_SEQ - 16, 0)

    d_rows = [dot_back(d_pre_a, wa[h]) + dot_back(d_pre_b, wb[h]) for h in (0, 1)]
    sums = scatter_z(z, d_rows[0], d_rows[1])
    d_inputs = norm_back_one(scal, d_x_one, x, sums, g_one)
    total_b = add_low(*outer_core(rows_one, d_pre_b))

    d_g_one = [
        jnp.sum(d_rows[h] * rows_one[h].astype(F32), axis=0, keepdims=True) for h in (0, 1)
    ]
    d_g_one = from_relative_gain(scal, *d_g_one) / g_one

    def gate_grads(k):
        part = slice(k * CH, (k + 1) * CH)
        both = [dot_outer(xg[:, part], g[:, part]) for g in (d_pre_r, d_pre_i)]
        return jnp.stack([v[q : q + 192, q : q + 192] for v in both for q in (0, 192)])

    def small_rows(k):
        return jnp.concatenate(
            [
                gate_grads(k).reshape(2, 192, CH),
                sums8[:, k * CH : (k + 1) * CH].reshape(2, 4, CH),
                gain_rows,
            ],
            axis=1,
        ).astype(BF16)

    gains = jnp.concatenate([d_g_one, d_g_two], axis=1).reshape(-1)
    gain_rows = jnp.concatenate([gains, jnp.zeros((4608 - 4096,), F32)]).reshape(2, 6, CH)
    small = jnp.stack([small_rows(0), small_rows(1)], axis=1)
    kept = lax.dynamic_index_in_dim(small, core, 0, keepdims=False)
    given = lax.dynamic_index_in_dim(small, 1 - core, 0, keepdims=False)

    kept = add_low(kept, swap_send(given, CORE))
    kept = add_low(kept[0], swap_send(kept[1], 4))
    kept = tie(kept, total_b)
    kept = add_low(kept, swap_send(kept, 64))
    b_stage = first_x(tie(total_b, kept))
    (d_w_b,) = finish(b_stage, False)
    kept = add_low(kept, swap_send(kept, 16))
    d_w_gate, d_w_up, d_w_down = finish_mlp(tie(shards, kept))
    kept = add_low(kept, swap_send(kept, 32))
    back = swap_send(kept, CORE)
    small = jnp.where(core == 0, jnp.stack([kept, back]), jnp.stack([back, kept])).astype(F32)
    d_gates = small[:, :192].reshape(2, 2, 192, 192)
    sums8 = small[:, 192:196].reshape(8, CH)
    gains = small[:, 196:].reshape(-1)[:4096].reshape(2, 2048)
    for mask in (1, 2):
        gains = gains + swap_send(gains, mask)

    in_second = (length > HALF_SEQ).astype(jnp.int32)
    window = lax.dynamic_slice_in_dim(ext, 5 + jnp.clip(length - HALF_SEQ * x_lo, 0, HALF_SEQ), 3, 0)
    window = jnp.where(x_lo == in_second, window, 0.0)
    state = jnp.where(first_half, 0.0, final[:1])
    ends = jnp.concatenate([window, state], axis=0)
    ends = ends[:, :CH] + swap_send(ends[:, CH:], 4)

    return (
        result[None],
        ends[3:4],
        ends[None, :3],
        d_inputs[None],
        gains[0],
        d_w_a,
        d_w_b,
        sums8[0:4],
        sums8[4],
        d_gates[0],
        d_gates[1],
        sums8[5],
        sums8[6],
        sums8[7],
        d_w_out,
        gains[1],
        d_w_gate,
        d_w_up,
        d_w_down,
    )


def solution(mesh):
    return jax.shard_map(
        on_device,
        mesh=mesh,
        in_specs=(
            P("dp", "mp", None),
            P("dp"),
            P("mp"),
            P("dp", "mp"),
            P("dp", None, "mp"),
            P(),
            P("dp", "mp"),
            P("dp", "mp"),
            P(None, "mp"),
            P("mp"),
            P("mp", None, None),
            P("mp", None, None),
            P("mp"),
            P("mp"),
            P("mp"),
            P("mp", "dp"),
            P(),
            P("dp", "mp"),
            P("dp", "mp"),
            P("mp", "dp"),
            P("dp", "mp", None),
        ),
        out_specs=(
            P("dp", "mp", None),
            P("dp", "mp"),
            P("dp", None, "mp"),
            P("dp", "mp", None),
            P(),
            P("dp", "mp"),
            P("dp", "mp"),
            P(None, "mp"),
            P("mp"),
            P("mp", None, None),
            P("mp", None, None),
            P("mp"),
            P("mp"),
            P("mp"),
            P("mp", "dp"),
            P(),
            P("dp", "mp"),
            P("dp", "mp"),
            P("mp", "dp"),
        ),
        check_vma=False,
    )
```

```python
import functools

import jax
import jax.numpy as jnp
from jax import lax
from jax.experimental import pallas as pl
from jax.experimental.pallas import tpu as pltpu
from jax.sharding import PartitionSpec as P

EPS = 1e-06
F32 = jnp.float32
BF16 = jnp.bfloat16
AXES = ("dp", "mp")
DEVICES = 128

Z_MASKS = (0, 1, 2, 3)
X_MASKS = (0, 4, 64, 68)
Y_MASKS = (0, 16, 32, 48)
CORE = 8
HALF_SEQ = 512
TOK = 128
CH = 384
WIDE = 768
CHUNKS = 8
STEPS = 64
GELU_A = 0.7978845608028654
GELU_B = 0.044715


def swap_send(values, mask):
    return lax.ppermute(values, AXES, [(i, i ^ mask) for i in range(DEVICES)])


def block_of(position, dp):
    mirrored = (position & 6) | ((position & 1) << 3) | ((position >> 3) & 1)
    return dp ^ mirrored


def gelu_parts(v):
    inner = GELU_A * (v + GELU_B * v * v * v)
    t = jnp.tanh(inner)
    half = 0.5 * (1.0 + t)
    slope = half + 0.5 * v * (1.0 - t * t) * (GELU_A * (1.0 + (3.0 * GELU_B) * v * v))
    return v * half, slope


def gelu_value(v):
    return v * (0.5 * (1.0 + jnp.tanh(GELU_A * (v + GELU_B * v * v * v))))


def neg_expm1(v):
    series = 1.0 + v * (1.0 / 9.0)
    for n in range(8, 1, -1):
        series = 1.0 + (v * (1.0 / n)) * series
    return jnp.where(v > -0.5, -v * series, 1.0 - jnp.exp(v))


def vmem(limit):
    return pltpu.CompilerParams(vmem_limit_bytes=limit * 1024 * 1024)


SMEM_SPEC = pl.BlockSpec(memory_space=pltpu.SMEM)


def block_rows(dp, p):
    return pl.ds(pl.multiple_of(block_of(p, dp) * 128, 128), 128)


def cols(p):
    return slice(p * 128, (p + 1) * 128)


def prep_kernel(scal, x_ref, g_ref, n_ref):
    dp = scal[2]
    x = x_ref[...].astype(F32)
    s = lax.rsqrt(jnp.mean(x * x, axis=-1, keepdims=True) + EPS)
    for p in range(16):
        src = block_rows(dp, p)
        n_ref[:, cols(p)] = (x_ref[:, src].astype(F32) * s * g_ref[:, src]).astype(BF16)


def prep(scal, x, g):
    return pl.pallas_call(
        prep_kernel,
        out_shape=jax.ShapeDtypeStruct((TOK, 2048), BF16),
        in_specs=[SMEM_SPEC] + [pl.BlockSpec(memory_space=pltpu.VMEM)] * 2,
        compiler_params=vmem(16),
        name="prep",
    )(scal, x, g)


def to_relative_kernel(scal, rows_ref, out0, out1):
    for p in range(16):
        out = (out0, out1)[p // 8]
        out[:, cols(p % 8)] = rows_ref[:, block_rows(scal[2], p)]


def to_relative(scal, rows):
    n = rows.shape[0]
    return pl.pallas_call(
        to_relative_kernel,
        grid=(2,),
        out_shape=(jax.ShapeDtypeStruct((n, 1024), rows.dtype),) * 2,
        in_specs=[SMEM_SPEC, pl.BlockSpec((n // 2, 2048), lambda i: (i, 0))],
        out_specs=(pl.BlockSpec((n // 2, 1024), lambda i: (i, 0)),) * 2,
        compiler_params=vmem(16),
        name="to_relative",
    )(scal, rows)


def gain_kernel(scal, in0, in1, out):
    for p in range(16):
        out[:, block_rows(scal[2], p)] = (in0, in1)[p // 8][:, cols(p % 8)]


def from_relative_gain(scal, g0, g1):
    return pl.pallas_call(
        gain_kernel,
        out_shape=jax.ShapeDtypeStruct((1, 2048), F32),
        in_specs=[SMEM_SPEC] + [pl.BlockSpec(memory_space=pltpu.VMEM)] * 2,
        name="gain_order",
    )(scal, g0, g1)


def assemble_kernel(scal, own, p1, p2_0, p2_1, p3, *outs):
    z = scal[0]
    for j, block in enumerate((own, p1, None, p3)):
        rows = pl.ds(pl.multiple_of((z ^ j) * TOK, TOK), TOK)
        for h in (0, 1):
            part = slice(h * 1024, (h + 1) * 1024)
            value = (p2_0, p2_1)[h][...] if block is None else block[:, part]
            if len(outs) == 2:
                outs[h][rows, :] = value
            else:
                outs[0][rows, part] = value


def assemble(scal, blocks, halves):
    shape = jax.ShapeDtypeStruct((HALF_SEQ, 1024 if halves else 2048), BF16)
    return pl.pallas_call(
        assemble_kernel,
        out_shape=(shape, shape) if halves else shape,
        in_specs=[SMEM_SPEC] + [pl.BlockSpec(memory_space=pltpu.VMEM)] * 5,
        compiler_params=vmem(16),
        name="assemble",
    )(scal, *blocks)


def add_blocks(dp, sums, base, out):
    own0, own1, a, b = sums
    for p in range(16):
        own = (own0, own1)[p // 8][:, cols(p % 8)]
        dst = block_rows(dp, p)
        total = own + a[:, cols(p)].astype(F32) + b[:, cols(p)].astype(F32)
        out[:, dst] = total if base is None else base[:, dst].astype(F32) + total


def mid_kernel(scal, x_ref, own0, own1, a, b, g_ref, xo_ref, n_ref):
    add_blocks(scal[2], (own0, own1, a, b), x_ref, xo_ref)
    x = xo_ref[...]
    s = lax.rsqrt(jnp.mean(x * x, axis=-1, keepdims=True) + EPS)
    n_ref[...] = (x * s * g_ref[...]).astype(BF16)


def mid_norm(scal, x, sums, g):
    return pl.pallas_call(
        mid_kernel,
        out_shape=(
            jax.ShapeDtypeStruct((TOK, 2048), F32),
            jax.ShapeDtypeStruct((TOK, 2048), BF16),
        ),
        in_specs=[SMEM_SPEC] + [pl.BlockSpec(memory_space=pltpu.VMEM)] * 6,
        compiler_params=vmem(16),
        name="mid_norm",
    )(scal, x, *sums, g)


def norm_gradient(x, g, dn):
    s = lax.rsqrt(jnp.mean(x * x, axis=-1, keepdims=True) + EPS)
    w = g * dn
    inner = jnp.mean(w * x, axis=-1, keepdims=True)
    return s * (w - x * (s * s * inner)), s


def back_two_kernel(scal, c_ref, x_ref, own0, own1, a, b, g_ref, dx_ref, dm_ref, dg_ref):
    own = jnp.concatenate([own0[...], own1[...]], axis=1)
    dn = own + a[...].astype(F32) + b[...].astype(F32)
    x = x_ref[...]
    back, s = norm_gradient(x, g_ref[...], dn)
    dg_ref[...] = jnp.sum(dn * x * s, axis=0, keepdims=True)
    dx_ref[...] = c_ref[...].astype(F32) + back
    for p in range(16):
        dm_ref[:, cols(p)] = dx_ref[:, block_rows(scal[2], p)].astype(BF16)


def norm_back_two(scal, c, x, sums, g):
    return pl.pallas_call(
        back_two_kernel,
        out_shape=(
            jax.ShapeDtypeStruct((TOK, 2048), F32),
            jax.ShapeDtypeStruct((TOK, 2048), BF16),
            jax.ShapeDtypeStruct((1, 2048), F32),
        ),
        in_specs=[SMEM_SPEC] + [pl.BlockSpec(memory_space=pltpu.VMEM)] * 7,
        compiler_params=vmem(24),
        name="norm_back_two",
    )(scal, c, x, *sums, g)


def back_one_kernel(scal, base_ref, x_ref, own0, own1, a, b, g_ref, dx_ref, dn_ref):
    add_blocks(scal[2], (own0, own1, a, b), None, dn_ref)
    back, _ = norm_gradient(x_ref[...].astype(F32), g_ref[...], dn_ref[...])
    dx_ref[...] = base_ref[...] + back


def norm_back_one(scal, base, x, sums, g):
    return pl.pallas_call(
        back_one_kernel,
        out_shape=jax.ShapeDtypeStruct((TOK, 2048), F32),
        in_specs=[SMEM_SPEC] + [pl.BlockSpec(memory_space=pltpu.VMEM)] * 7,
        scratch_shapes=[pltpu.VMEM((TOK, 2048), F32)],
        compiler_params=vmem(24),
        name="norm_back_one",
    )(scal, base, x, *sums, g)


PACK_ROWS = 16
ROW_CB, ROW_BR, ROW_BI, ROW_DECAY, ROW_MASK, ROW_H, ROW_SIG = 4, 5, 6, 7, 8, 9, 10


def row(ref, i):
    return ref[i : i + 1, :]


def valid_rows(scal, start, size):
    t = lax.broadcasted_iota(jnp.int32, (size, 1), 0) + (scal[1] * HALF_SEQ + start)
    return t < scal[3]


GROUPS = 3


def pack_kernel(sizes, cw, cb, br, bi, lam, h, cs, out):
    slot = lax.broadcasted_iota(jnp.int32, (1, CH), 1)
    limit = jnp.where(slot < 192, sizes[0], 192 + sizes[1])
    mask = jnp.where(slot < limit, 1.0, 0.0)
    out[...] = jnp.zeros_like(out)
    out[0:4, :] = cw[...]
    out[ROW_CB : ROW_CB + 1, :] = cb[...]
    out[ROW_BR : ROW_BR + 1, :] = br[...]
    out[ROW_BI : ROW_BI + 1, :] = bi[...]
    out[ROW_DECAY : ROW_DECAY + 1, :] = -8.0 * jax.nn.softplus(-lam[...])
    out[ROW_MASK : ROW_MASK + 1, :] = mask
    out[ROW_H : ROW_H + 1, :] = h[...] * mask
    out[ROW_SIG : ROW_SIG + 1, :] = jax.nn.sigmoid(-lam[...])
    out[11:14, :] = cs[...] * mask


def make_pack(head_sizes, *rows):
    return pl.pallas_call(
        pack_kernel,
        out_shape=jax.ShapeDtypeStruct((PACK_ROWS, CH), F32),
        in_specs=[SMEM_SPEC] + [pl.BlockSpec(memory_space=pltpu.VMEM)] * 7,
        name="pack",
    )(head_sizes, *rows)


def put(ref, rows, value):
    for g in range(GROUPS):
        ref[g, rows, :] = value[:, g * 128 : (g + 1) * 128]


def take(ref, rows):
    return jnp.concatenate([ref[g, rows, :] for g in range(GROUPS)], axis=1)


def at_step(ref, s):
    rows = pl.ds(s, CHUNKS, stride=STEPS)
    return [ref.at[g][rows, :] for g in range(GROUPS)]


def put_step(ref, s, values):
    rows = pl.ds(s, CHUNKS, stride=STEPS)
    for g in range(GROUPS):
        ref.at[g][rows, :] = values[g]


def run_steps(step):
    start = [jnp.zeros((CHUNKS, 128), F32)] * GROUPS + [jnp.ones((CHUNKS, 128), F32)] * GROUPS
    out = lax.fori_loop(0, STEPS, step, tuple(start), unroll=4)
    return jnp.concatenate(out[:GROUPS], axis=1), jnp.concatenate(out[GROUPS:], axis=1)


def mix_fwd_kernel(
    scal, pre_b, halo, par, wr, wi, rate, inlet, conv, xg, av, hl, pcum, ext, end, bv
):
    mask = row(par, ROW_MASK)
    ext[0:8, :] = halo[...]
    for c in range(CHUNKS):
        ext[8 + c * STEPS : 8 + (c + 1) * STEPS, :] = pre_b[c * STEPS : (c + 1) * STEPS, :] * mask
    for c in range(CHUNKS):
        t0 = c * STEPS
        acc = row(par, ROW_CB) + row(par, 0) * ext[t0 + 5 : t0 + 5 + STEPS, :]
        for k in range(1, 4):
            acc = acc + row(par, k) * ext[t0 + 5 + k : t0 + 5 + k + STEPS, :]
        acc = acc * mask
        conv[t0 : t0 + STEPS, :] = acc
        xg[t0 : t0 + STEPS, :] = acc.astype(BF16)
    rate[...] = jnp.dot(xg[...], wr[0], preferred_element_type=F32)
    inlet[...] = jnp.dot(xg[...], wi[0], preferred_element_type=F32)
    for c in range(CHUNKS):
        rows = slice(c * STEPS, (c + 1) * STEPS)
        r = jax.nn.sigmoid(rate[rows, :] + row(par, ROW_BR))
        i = jax.nn.sigmoid(inlet[rows, :] + row(par, ROW_BI))
        rate[rows, :] = r
        inlet[rows, :] = i
        log_a = row(par, ROW_DECAY) * r
        mult = jnp.sqrt(neg_expm1(2.0 * log_a))
        valid = valid_rows(scal, c * STEPS, STEPS)
        put(av, rows, jnp.where(valid, jnp.exp(log_a), 1.0))
        put(bv, rows, jnp.where(valid, mult * i * conv[rows, :], 0.0))

    def step(s, carry):
        a, b = at_step(av, s), at_step(bv, s)
        h = [a[g] * carry[g] + b[g] for g in range(GROUPS)]
        p = [a[g] * carry[GROUPS + g] for g in range(GROUPS)]
        put_step(hl, s, h)
        put_step(pcum, s, p)
        return tuple(h + p)

    h, p = run_steps(step)
    carry = row(par, ROW_H)
    for c in range(CHUNKS):
        carry = h[c : c + 1, :] + p[c : c + 1, :] * carry
    end[...] = jnp.broadcast_to(carry, (8, CH))


def wide(rows):
    return pl.BlockSpec((rows, CH), lambda i: (0, i))


GATE_SPEC = pl.BlockSpec((1, CH, CH), lambda i: (i, 0, 0))


STRIP_SPEC = pl.BlockSpec((GROUPS, 512, 128), lambda i: (i, 0, 0))
STRIP = jax.ShapeDtypeStruct((2 * GROUPS, 512, 128), F32)
STRIP_SCRATCH = pltpu.VMEM((GROUPS, 512, 128), F32)


def sds(rows, dtype=F32):
    return jax.ShapeDtypeStruct((rows, WIDE), dtype)


def mix_fwd(scal, pre_b, halo, par, wr, wi):
    return pl.pallas_call(
        mix_fwd_kernel,
        grid=(2,),
        out_shape=(
            sds(512), sds(512), sds(512), sds(512, BF16), STRIP, STRIP, STRIP, sds(520), sds(8),
        ),
        in_specs=[SMEM_SPEC, wide(512), wide(8), wide(16), GATE_SPEC, GATE_SPEC],
        out_specs=(
            wide(512), wide(512), wide(512), wide(512), STRIP_SPEC, STRIP_SPEC, STRIP_SPEC, wide(520), wide(8),
        ),
        scratch_shapes=[STRIP_SCRATCH],
        compiler_params=vmem(32),
        name="mix_fwd",
    )(scal, pre_b, halo, par, wr, wi)


def mix_out_kernel(scal, hl, pcum, pre_a, h_in, h_ext, mixed, final):
    h_ext[0:8, :] = h_in[...]
    carry = row(h_in, 7)
    for c in range(CHUNKS):
        rows = slice(c * STEPS, (c + 1) * STEPS)
        h = take(hl, rows) + take(pcum, rows) * carry
        h_ext[8 + c * STEPS : 8 + (c + 1) * STEPS, :] = h
        carry = h[STEPS - 1 : STEPS, :]
        mixed[rows, :] = (gelu_value(pre_a[rows, :]) * h).astype(BF16)
    final[...] = jnp.broadcast_to(carry, (8, CH))


def mix_out(scal, hl, pcum, pre_a, h_in):
    return pl.pallas_call(
        mix_out_kernel,
        grid=(2,),
        out_shape=(sds(520), sds(512, BF16), sds(8)),
        in_specs=[SMEM_SPEC, STRIP_SPEC, STRIP_SPEC, wide(512), wide(8)],
        out_specs=(wide(520), wide(512), wide(8)),
        compiler_params=vmem(32),
        name="mix_out",
    )(scal, hl, pcum, pre_a, h_in)


def mix_back_kernel(scal, d_mix, pre_a, h_ext, av, d_pre_a, rl, qcum, end, dh):
    for c in range(CHUNKS):
        rows = slice(c * STEPS, (c + 1) * STEPS)
        act, slope = gelu_parts(pre_a[rows, :])
        dm = d_mix[rows, :]
        h = h_ext[8 + c * STEPS : 8 + (c + 1) * STEPS, :]
        d_pre_a[rows, :] = (slope * h * dm).astype(BF16)
        put(dh, rows, dm * act)

    def step(n, carry):
        s = STEPS - 1 - n
        a, d = at_step(av, s), at_step(dh, s)
        carried = [d[g] + carry[g] for g in range(GROUPS)]
        put_step(rl, s, carried)
        put_step(qcum, s, carry[GROUPS:])
        u = [a[g] * carried[g] for g in range(GROUPS)]
        return tuple(u + [a[g] * carry[GROUPS + g] for g in range(GROUPS)])

    u, q = run_steps(step)
    carry = jnp.zeros((1, CH), F32)
    for c in range(CHUNKS - 1, -1, -1):
        carry = u[c : c + 1, :] + q[c : c + 1, :] * carry
    end[...] = jnp.broadcast_to(carry, (8, CH))


def mix_back(scal, d_mix, pre_a, h_ext, av):
    return pl.pallas_call(
        mix_back_kernel,
        grid=(2,),
        out_shape=(sds(512, BF16), STRIP, STRIP, sds(8)),
        in_specs=[SMEM_SPEC, wide(512), wide(512), wide(520), STRIP_SPEC],
        out_specs=(wide(512), STRIP_SPEC, STRIP_SPEC, wide(8)),
        scratch_shapes=[STRIP_SCRATCH],
        compiler_params=vmem(32),
        name="mix_back",
    )(scal, d_mix, pre_a, h_ext, av)


def total_rows(v):
    return jnp.sum(v, axis=0, keepdims=True)


def mix_grad_kernel(
    scal, rl, qcum, av, u_in, rate, inlet, conv, h_ext, ext, par, wr, wi,
    d_pre_r, d_pre_i, d_pre_b, tail, head, sums, dconv,
):
    mask = row(par, ROW_MASK)
    carry = row(u_in, 0)
    d_lam = jnp.zeros((1, CH), F32)
    d_br = jnp.zeros((1, CH), F32)
    d_bi = jnp.zeros((1, CH), F32)
    for c in range(CHUNKS - 1, -1, -1):
        t0 = c * STEPS
        rows = slice(t0, t0 + STEPS)
        a = take(av, rows)
        carried = take(rl, rows) + take(qcum, rows) * carry
        carry = a[0:1, :] * carried[0:1, :]
        valid = valid_rows(scal, t0, STEPS)
        d_drive = jnp.where(valid, carried, 0.0)
        d_decay = d_drive * h_ext[t0 + 7 : t0 + 7 + STEPS, :]
        r, i, x = rate[rows, :], inlet[rows, :], conv[rows, :]
        gap = neg_expm1(2.0 * (row(par, ROW_DECAY) * r))
        inv = lax.rsqrt(gap)
        mult = gap * inv
        driven = d_drive * i
        d_log = d_decay * a - driven * x * (a * a) * inv
        d_lam = d_lam + total_rows(d_log * r)
        pr = (d_log * row(par, ROW_DECAY) * r * (1.0 - r)).astype(BF16)
        pi = (d_drive * mult * x * i * (1.0 - i)).astype(BF16)
        d_pre_r[rows, :] = pr
        d_pre_i[rows, :] = pi
        d_br = d_br + total_rows(pr.astype(F32))
        d_bi = d_bi + total_rows(pi.astype(F32))
        dconv[rows, :] = driven * mult
    dims = (((1,), (1,)), ((), ()))
    gate = lax.dot_general(d_pre_r[...], wr[0], dims, preferred_element_type=F32)
    gate = gate + lax.dot_general(d_pre_i[...], wi[0], dims, preferred_element_type=F32)
    dconv[0:HALF_SEQ, :] = (dconv[0:HALF_SEQ, :] + gate) * mask
    dconv[HALF_SEQ : HALF_SEQ + 8, :] = jnp.zeros((8, CH), F32)
    head[...] = dconv[0:8, :]
    taps = [jnp.zeros((1, CH), F32) for _ in range(4)]
    bias = jnp.zeros((1, CH), F32)
    for c in range(CHUNKS):
        t0 = c * STEPS
        here = dconv[t0 : t0 + STEPS, :]
        bias = bias + total_rows(here)
        back = jnp.zeros((STEPS, CH), F32)
        for k in range(4):
            taps[k] = taps[k] + total_rows(here * ext[t0 + 5 + k : t0 + 5 + k + STEPS, :])
            back = back + row(par, k) * dconv[t0 + 3 - k : t0 + 3 - k + STEPS, :]
        back = back * mask
        d_pre_b[t0 : t0 + STEPS, :] = back.astype(BF16)
        if c == CHUNKS - 1:
            tail[...] = back[STEPS - 16 :, :]
    for k in range(4):
        sums[k : k + 1, :] = taps[k]
    sums[4:5, :] = bias
    sums[5:6, :] = d_br
    sums[6:7, :] = d_bi
    sums[7:8, :] = 8.0 * row(par, ROW_SIG) * d_lam


def mix_grad(scal, rl, qcum, av, u_in, rate, inlet, conv, h_ext, ext, par, wr, wi):
    return pl.pallas_call(
        mix_grad_kernel,
        grid=(2,),
        out_shape=(sds(512, BF16), sds(512, BF16), sds(512, BF16), sds(16), sds(8), sds(8)),
        in_specs=[
            SMEM_SPEC, STRIP_SPEC, STRIP_SPEC, STRIP_SPEC, wide(8), wide(512), wide(512), wide(512),
            wide(520), wide(520), wide(16), GATE_SPEC, GATE_SPEC,
        ],
        out_specs=(wide(512), wide(512), wide(512), wide(16), wide(8), wide(8)),
        scratch_shapes=[pltpu.VMEM((HALF_SEQ + 8, CH), F32)],
        compiler_params=vmem(40),
        name="mix_grad",
    )(scal, rl, qcum, av, u_in, rate, inlet, conv, h_ext, ext, par, wr, wi)


def tie(values, *earlier):
    return lax.optimization_barrier((values, earlier))[0]


def gather_z(own):
    p1 = swap_send(own, 1)
    p3 = swap_send(own, 3)
    p2_0 = swap_send(p3[:, :1024], 1)
    p2_1 = swap_send(p1[:, 1024:], 3)
    return own, p1, p2_0, p2_1, p3


def far_blocks(z, part0, part1):
    return [
        lax.dynamic_slice_in_dim(p, (z ^ 2) * TOK, TOK, 0).astype(BF16) for p in (part0, part1)
    ]


def scatter_z(z, part0, part1, far=None):
    def block(part, j):
        return lax.dynamic_slice_in_dim(part, (z ^ j) * TOK, TOK, 0)

    far = far or far_blocks(z, part0, part1)
    far_0 = swap_send(far[0], 1)
    far_1 = swap_send(far[1], 3)
    to_1 = [block(part0, 1).astype(BF16), (block(part1, 1) + far_1.astype(F32)).astype(BF16)]
    to_3 = [(block(part0, 3) + far_0.astype(F32)).astype(BF16), block(part1, 3).astype(BF16)]
    r1 = swap_send(jnp.concatenate(to_1, axis=1), 1)
    r3 = swap_send(jnp.concatenate(to_3, axis=1), 3)
    return block(part0, 0), block(part1, 0), r1, r3


Z_GROUPS = [[0, 1, 2, 3], [4, 5, 6, 7]]


def reduce_z(values):
    return lax.psum_scatter(
        values, "mp", scatter_dimension=0, axis_index_groups=Z_GROUPS, tiled=True
    )


def cross(axis, blocks):
    return jnp.concatenate(
        [
            jnp.concatenate([blocks[0], blocks[1]], axis=-1),
            jnp.concatenate([blocks[2], blocks[3]], axis=-1),
        ],
        axis=axis,
    )


def join_mixer_kernel(*refs):
    one, two, out = refs[:4], refs[4:8], refs[8]
    for y in range(4):
        rows = slice(y * 256, (y + 1) * 256)
        out[rows, :CH] = one[y][:, :CH]
        out[rows, CH:WIDE] = one[y][:, 512 : 512 + CH]
        out[rows, 2 * WIDE : 2 * WIDE + 128] = one[y][:, CH:512]
        out[rows, 2 * WIDE + CH : 2 * WIDE + CH + 128] = one[y][:, 512 + CH :]
        for r in (0, 1):
            rows = slice(y * 256 + r * 128, y * 256 + (r + 1) * 128)
            own, other = two[2 * r], two[2 * r + 1]
            out[rows, WIDE : WIDE + CH] = own[y, :, :CH]
            out[rows, WIDE + CH : 2 * WIDE] = other[y, :, :CH]
            out[rows, 2 * WIDE + 128 : 2 * WIDE + CH] = own[y, :, CH:]
            out[rows, 2 * WIDE + CH + 128 :] = other[y, :, CH:]


def join_mixer(one, two):
    return pl.pallas_call(
        join_mixer_kernel,
        out_shape=jax.ShapeDtypeStruct((1024, 3 * WIDE), BF16),
        compiler_params=vmem(24),
        name="join_mixer",
    )(*one, *two)


def sum_four(own, a, b, c):
    return (own.astype(F32) + a.astype(F32)) + (b.astype(F32) + c.astype(F32))


def add_low(a, b):
    return (a.astype(F32) + b.astype(F32)).astype(BF16)


def y_pieces(total):
    return [total[k * 256 : (k + 1) * 256] for k in range(4)]


def x_pieces(total):
    n = total.shape[-1] // 2
    return [total[:, r * 128 : (r + 1) * 128, c * n : (c + 1) * n] for r in (0, 1) for c in (0, 1)]


def send_three(pieces, masks):
    return [swap_send(v, m) for v, m in zip(pieces[1:], masks[1:])]


def first_y(total):
    py = y_pieces(total)
    received = send_three(py, Y_MASKS)
    pieces = [v[0] for v in x_pieces(sum_four(py[0], *received).astype(BF16)[None])]
    return received, pieces, X_MASKS


def first_x(total):
    px = x_pieces(total.reshape(4, 256, -1))
    received = send_three(px, X_MASKS)
    total = sum_four(px[0], *received).astype(BF16)
    return received, [total[k] for k in range(4)], Y_MASKS


def finish_kernel(*refs, turned):
    total = sum_four(*[r[...] for r in refs[:4]])
    at = 0
    for out, turn in zip(refs[4:], turned):
        n = out.shape[0] if turn else out.shape[1]
        part = total[:, at : at + n]
        out[...] = part.T if turn else part
        at += n


def finish(stage, *turned):
    _, pieces, masks = stage
    terms = [pieces[0]] + send_three(pieces, masks)
    n = pieces[0].shape[1] // len(turned)
    shapes = [jax.ShapeDtypeStruct((n, TOK) if t else (TOK, n), F32) for t in turned]
    return pl.pallas_call(
        functools.partial(finish_kernel, turned=turned),
        out_shape=tuple(shapes),
        compiler_params=vmem(16),
        name="finish",
    )(*terms)


def outer_mlp_kernel(n_ref, c_ref, gu_ref, h_ref, out_ref, turned):
    step = pl.program_id(0)

    @pl.when(step == 0)
    def _():
        turned[...] = n_ref[...].T

    @pl.when(step == 6)
    def _():
        turned[...] = c_ref[...].T

    @pl.when(step < 6)
    def _():
        out_ref[...] = jnp.dot(turned[...], gu_ref[...], preferred_element_type=F32).astype(BF16)

    @pl.when(step >= 6)
    def _():
        out_ref[...] = jnp.dot(turned[...], h_ref[...], preferred_element_type=F32).astype(BF16)


def outer_mlp(rows_two, rows_c, d_gate_up, hidden):
    whole = pl.BlockSpec((HALF_SEQ, 2048), lambda i: (0, 0))
    return pl.pallas_call(
        outer_mlp_kernel,
        grid=(9,),
        out_shape=jax.ShapeDtypeStruct((2048, 6 * WIDE), BF16),
        in_specs=[
            whole,
            whole,
            pl.BlockSpec((HALF_SEQ, 512), lambda i: (0, jnp.minimum(i, 5))),
            pl.BlockSpec((HALF_SEQ, 512), lambda i: (0, jnp.maximum(i - 6, 0))),
        ],
        out_specs=pl.BlockSpec((2048, 512), lambda i: (0, i)),
        scratch_shapes=[pltpu.VMEM((2048, HALF_SEQ), BF16)],
        compiler_params=vmem(40),
        cost_estimate=pl.CostEstimate(
            flops=2 * 2048 * 4608 * 512, bytes_accessed=30 * 2**20, transcendentals=0
        ),
        name="outer_mlp",
    )(rows_two, rows_c, d_gate_up, hidden)


def finish_mlp_kernel(mine, other, gate, up, down):
    for k, out in enumerate((gate, up)):
        own = mine[:, 2 * k * WIDE : (2 * k + 1) * WIDE]
        out[...] = own.astype(F32) + other[:, k * WIDE : (k + 1) * WIDE].astype(F32)
    own = mine[:, 4 * WIDE : 5 * WIDE]
    down[...] = (own.astype(F32) + other[:, 2 * WIDE :].astype(F32)).T


def send_mlp(shards):
    given = [shards[:, k * WIDE : (k + 1) * WIDE] for k in (1, 3, 5)]
    return swap_send(jnp.concatenate(given, axis=1), 4)


def finish_mlp(shards, received):
    shape = jax.ShapeDtypeStruct((TOK, WIDE), F32)
    return pl.pallas_call(
        finish_mlp_kernel,
        out_shape=(shape, shape, jax.ShapeDtypeStruct((WIDE, TOK), F32)),
        compiler_params=vmem(16),
        name="finish_mlp",
    )(shards, received)


def swap_channels(v):
    return jnp.concatenate([v[..., CH:], v[..., :CH]], axis=-1)


def dot(a, b):
    return jnp.dot(a, b, preferred_element_type=F32)


def dot_back(a, b):
    return lax.dot_general(a, b, (((1,), (1,)), ((), ())), preferred_element_type=F32)


def dot_outer(a, b):
    return lax.dot_general(a, b, (((0,), (0,)), ((), ())), preferred_element_type=F32)


def pair_blocks(w):
    zero = jnp.zeros_like(w[..., 0, :, :])
    top = jnp.concatenate([w[..., 0, :, :], zero], axis=-1)
    low_rows = jnp.concatenate([zero, w[..., 1, :, :]], axis=-1)
    return jnp.concatenate([top, low_rows], axis=-2)


def on_device(
    inputs,
    lengths,
    head_sizes,
    h_start,
    conv_start,
    g_one,
    w_a,
    w_b,
    conv_w,
    conv_b,
    w_r,
    w_i,
    b_r,
    b_i,
    lam,
    w_out,
    g_two,
    w_gate,
    w_up,
    w_down,
    cotangent,
):
    dp = lax.axis_index("dp").astype(jnp.int32)
    mp = lax.axis_index("mp").astype(jnp.int32)
    z, x_lo, core = mp % 4, mp // 4, dp % 2
    length = lengths[0]
    scal = jnp.stack([z, x_lo, dp, length])
    first_half = x_lo == 0
    g_one, g_two = g_one[None], g_two[None]

    shard = jnp.concatenate([w_gate, w_up, w_down.T], axis=1)

    out_t = w_out.T
    first = jnp.concatenate([w_a, out_t[:, :128]], axis=1)
    second = jnp.concatenate([w_b, out_t[:, 128:]], axis=1)
    gates = jnp.stack([w_r, w_i])
    y1, y3 = swap_send(second, 16), swap_send(second, 48)
    x3, x1 = swap_send(first, 68), swap_send(first, 4)
    x = inputs[0]
    c = cotangent[0]
    pack = make_pack(
        head_sizes, conv_w, conv_b[None], b_r[None], b_i[None], lam[None], h_start, conv_start[0]
    )
    pair = jnp.concatenate([shard, gates.reshape(TOK, 1152)], axis=1)
    far_first, far_second, pair = tie((first, second, pair), y1, y3, x1, x3)
    x2, y2 = swap_send(far_first, 64), swap_send(far_second, 32)
    pair = swap_send(pair, 4)
    n_one = tie(prep(scal, x, g_one), y1, y3, x1, x3)
    z1, z3 = swap_send(n_one, 1), swap_send(n_one, 3)
    pair = tie(pair, z1, z3)
    pack_other = swap_send(tie(pack, pair), 4)
    other, gates_other = pair[:, :2304], pair[:, 2304:]
    shard = jnp.concatenate(
        [v[:, i * WIDE : (i + 1) * WIDE] for i in range(3) for v in (shard, other)], axis=1
    )
    w_mlp = lax.all_gather(shard, "dp", axis=0, tiled=True)

    par = jnp.concatenate([pack, pack_other], axis=1)
    gates = pair_blocks(jnp.stack([gates, gates_other.reshape(gates.shape)], axis=1))
    wr, wi = gates[0], gates[1]
    rows = cross(0, [first, x1, x2, x3])
    stack = jnp.stack([second, y1, y2, y3], axis=0)
    rows, stack = tie((rows, stack), n_one, pack_other)
    ry1, ry3, sx2 = swap_send(rows, 16), swap_send(rows, 48), swap_send(stack, 64)
    z2_0, z2_1 = swap_send(z3[:, :1024], 1), swap_send(z1[:, 1024:], 3)
    far_rows, far_stack = tie((rows, stack), ry1, ry3, sx2, z1, z3)
    ry2, sx1, sx3 = swap_send(far_rows, 32), swap_send(far_stack, 4), swap_send(far_stack, 68)
    c_sent = tie(c, z1, z3)
    c1, c3 = swap_send(c_sent, 1), swap_send(c_sent, 3)
    ry2, sx1, sx3 = tie((ry2, sx1, sx3), z2_0, z2_1, c1, c3)
    mixer = join_mixer((rows, ry1, ry2, ry3), (stack, sx1, sx2, sx3))
    rows_one = assemble(scal, (n_one, z1, z2_0, z2_1, z3), True)
    mixers = (mixer, swap_send(mixer, CORE))
    wa = [m[:, :WIDE] for m in mixers]
    wb = [m[:, WIDE : 2 * WIDE] for m in mixers]
    wo = [m[:, 2 * WIDE :] for m in mixers]

    pre_b = dot(rows_one[0], wb[0]) + dot(rows_one[1], wb[1])
    edge = swap_channels(swap_send(pre_b[HALF_SEQ - 8 :], 4)) * par[ROW_MASK : ROW_MASK + 1]
    start_halo = jnp.concatenate([jnp.zeros((5, WIDE), F32), par[11:14]], axis=0)
    halo = jnp.where(first_half, start_halo, edge)
    par_used = par.at[ROW_H].set(jnp.where(first_half, par[ROW_H], 0.0))
    pre_a = dot(rows_one[0], wa[0]) + dot(rows_one[1], wa[1])
    rate, inlet, conv, xg, av, hl, pcum, ext, end = mix_fwd(scal, pre_b, halo, par_used, wr, wi)
    arrived = swap_channels(swap_send(end, 4))
    h_in = jnp.where(first_half, jnp.broadcast_to(par[ROW_H : ROW_H + 1], (8, WIDE)), arrived)
    c3_sent, c1_sent = tie((c3[:, :1024], c1[:, 1024:]), rows_one[0])
    c2_0, c2_1 = swap_send(c3_sent, 1), swap_send(c1_sent, 3)
    h_in = tie(h_in, c2_0, c2_1)
    h_ext, mixer_in, final = mix_out(scal, hl, pcum, pre_a, h_in)
    sums = scatter_z(z, dot_back(mixer_in, wo[0]), dot_back(mixer_in, wo[1]))
    rows_c = assemble(scal, (c, c1, c2_0, c2_1, c3), False)
    x_one, n_two = mid_norm(scal, x, sums, g_two)

    w_gate_up, w_dn = w_mlp[:, : 4 * WIDE], w_mlp[:, 4 * WIDE :]
    rows_two = assemble(scal, gather_z(n_two), False)
    gate_up = dot(rows_two, w_gate_up)
    d_hidden = dot(rows_c, w_dn)
    gate_pre, up_pre = gate_up[:, : 2 * WIDE], gate_up[:, 2 * WIDE :]
    act, slope = gelu_parts(gate_pre)
    hidden = (act * up_pre).astype(BF16)
    d_gate = (slope * (up_pre * d_hidden)).astype(BF16)
    d_up = (act * d_hidden).astype(BF16)
    d_gate_up = jnp.concatenate([d_gate, d_up], axis=1)
    d_rows = dot_back(d_gate_up, w_gate_up)
    d_rows = [d_rows[:, :1024], d_rows[:, 1024:]]
    far = far_blocks(z, *d_rows)
    d_w_mlp = outer_mlp(rows_two, rows_c, tie(d_gate_up, *d_rows), hidden)
    shards = lax.psum_scatter(d_w_mlp, "dp", scatter_dimension=0, tiled=True)
    sums = scatter_z(z, d_rows[0], d_rows[1], far)
    d_x_one, dm, d_g_two = norm_back_two(scal, c, x_one, sums, g_two)

    def outer_core(rows, grads):
        given, mine = [dot_outer(rows[h], grads).astype(BF16) for h in (1, 0)]
        return mine, swap_send(given, CORE)

    d_result = dot_back(tie(hidden, d_w_mlp), w_dn).astype(BF16)
    dm = tie(dm, d_result)

    rows_m = list(assemble(scal, gather_z(dm), True))
    d_mix = dot(rows_m[0], wo[0]) + dot(rows_m[1], wo[1])
    d_pre_a, rl, qcum, end = mix_back(scal, d_mix, pre_a, h_ext, av)
    arrived = swap_channels(swap_send(end, 4))
    u_in = jnp.where(first_half, arrived, 0.0)

    def own_first(o, a):
        return jnp.concatenate([o[:, :CH], a[:, :CH], o[:, CH:], a[:, CH:]], axis=1)

    oa = [
        own_first(
            dot_outer(rows_m[h], mixer_in).astype(BF16), dot_outer(rows_one[h], d_pre_a).astype(BF16)
        )
        for h in (0, 1)
    ]
    oa[1] = swap_send(oa[1], CORE)
    u_in = tie(u_in, oa[1])
    total_oa = add_low(*oa)
    oa = first_y(total_oa)
    d_pre_r, d_pre_i, d_pre_b, tail, head, sums8 = mix_grad(
        scal, rl, qcum, av, u_in, rate, inlet, conv, h_ext, ext, par, wr, wi
    )
    d_result = reduce_z(tie(d_result, head))
    result = (x_one + d_result.astype(F32)).astype(BF16)
    after = jnp.where(first_half, swap_channels(swap_send(head, 4)), 0.0)[:3]
    ahead = jnp.concatenate([jnp.zeros((16, WIDE), F32), after], axis=0)
    extra = par[0:1] * ahead[3:19]
    for k in range(1, 4):
        extra = extra + par[k : k + 1] * ahead[3 - k : 19 - k]
    tail = (tail + extra * par[ROW_MASK : ROW_MASK + 1]).astype(BF16)
    d_pre_b = lax.dynamic_update_slice_in_dim(d_pre_b, tail, HALF_SEQ - 16, 0)

    d_pre_b = tie(d_pre_b, total_oa)
    d_rows = [dot_back(d_pre_a, wa[h]) + dot_back(d_pre_b, wb[h]) for h in (0, 1)]
    sums = scatter_z(z, d_rows[0], d_rows[1])
    d_inputs = norm_back_one(scal, d_x_one, x, sums, g_one)
    d_g_one = [
        jnp.sum(d_rows[h] * rows_one[h].astype(F32), axis=0, keepdims=True) for h in (0, 1)
    ]
    d_g_one = from_relative_gain(scal, *d_g_one) / g_one

    def gate_grads(k):
        part = slice(k * CH, (k + 1) * CH)
        both = [dot_outer(xg[:, part], g[:, part]) for g in (d_pre_r, d_pre_i)]
        return jnp.stack([v[q : q + 192, q : q + 192] for v in both for q in (0, 192)])

    def small_rows(k):
        return jnp.concatenate(
            [
                gate_grads(k).reshape(2, 192, CH),
                sums8[:, k * CH : (k + 1) * CH].reshape(2, 4, CH),
                gain_rows,
            ],
            axis=1,
        ).astype(BF16)

    gains = jnp.concatenate([d_g_one, d_g_two], axis=0)
    for mask in (1, 2):
        gains = gains + swap_send(gains, mask)
    gains = gains.reshape(-1)
    gain_rows = jnp.concatenate([gains, jnp.zeros((4608 - 4096,), F32)]).reshape(2, 6, CH)
    small = jnp.stack([small_rows(0), small_rows(1)], axis=1)
    payload = small
    kept = lax.dynamic_index_in_dim(small, core, 0, keepdims=False)
    given = lax.dynamic_index_in_dim(small, 1 - core, 0, keepdims=False)

    kept = add_low(kept, swap_send(given, CORE))
    total_b = add_low(*outer_core(rows_one, tie(d_pre_b, small)))
    kept = tie(kept, total_b, *oa[0], *sums)
    kept = add_low(kept[0], swap_send(kept[1], 4))
    b_stage = first_y(total_b)
    received = send_mlp(tie(shards, kept))
    d_w_gate, d_w_up, d_w_down = finish_mlp(shards, received)
    kept = add_low(kept, swap_send(kept, 64))
    oa = (oa[0], tie(oa[1], kept), oa[2])
    d_w_out, d_w_a = finish(oa, True, False)
    kept = tie(kept, *b_stage[0])
    kept = add_low(kept, swap_send(kept, 16))
    kept = tie(kept, received)
    kept = add_low(kept, swap_send(kept, 32))
    (d_w_b,) = finish((b_stage[0], tie(b_stage[1], kept), b_stage[2]), False)
    back = swap_send(kept, CORE)
    small = jnp.where(core == 0, jnp.stack([kept, back]), jnp.stack([back, kept])).astype(F32)
    d_gates = small[:, :192].reshape(2, 2, 192, 192)
    sums8 = small[:, 192:196].reshape(8, CH)
    gains = small[:, 196:].reshape(-1)[:4096].reshape(2, 2048)

    in_second = (length > HALF_SEQ).astype(jnp.int32)
    window = lax.dynamic_slice_in_dim(ext, 5 + jnp.clip(length - HALF_SEQ * x_lo, 0, HALF_SEQ), 3, 0)
    window = jnp.where(x_lo == in_second, window, 0.0)
    state = jnp.where(first_half, 0.0, final[:1])
    ends = tie(jnp.concatenate([window, state], axis=0), payload)
    ends = ends[:, :CH] + swap_send(ends[:, CH:], 4)

    return (
        result[None],
        ends[3:4],
        ends[None, :3],
        d_inputs[None],
        gains[0],
        d_w_a,
        d_w_b,
        sums8[0:4],
        sums8[4],
        d_gates[0],
        d_gates[1],
        sums8[5],
        sums8[6],
        sums8[7],
        d_w_out,
        gains[1],
        d_w_gate,
        d_w_up,
        d_w_down,
    )


def solution(mesh):
    return jax.shard_map(
        on_device,
        mesh=mesh,
        in_specs=(
            P("dp", "mp", None),
            P("dp"),
            P("mp"),
            P("dp", "mp"),
            P("dp", None, "mp"),
            P(),
            P("dp", "mp"),
            P("dp", "mp"),
            P(None, "mp"),
            P("mp"),
            P("mp", None, None),
            P("mp", None, None),
            P("mp"),
            P("mp"),
            P("mp"),
            P("mp", "dp"),
            P(),
            P("dp", "mp"),
            P("dp", "mp"),
            P("mp", "dp"),
            P("dp", "mp", None),
        ),
        out_specs=(
            P("dp", "mp", None),
            P("dp", "mp"),
            P("dp", None, "mp"),
            P("dp", "mp", None),
            P(),
            P("dp", "mp"),
            P("dp", "mp"),
            P(None, "mp"),
            P("mp"),
            P("mp", None, None),
            P("mp", None, None),
            P("mp"),
            P("mp"),
            P("mp"),
            P("mp", "dp"),
            P(),
            P("dp", "mp"),
            P("dp", "mp"),
            P("mp", "dp"),
        ),
        check_vma=False,
    )
```

```python
import functools

import jax
import jax.numpy as jnp
from jax import lax
from jax.experimental import pallas as pl
from jax.experimental.pallas import tpu as pltpu
from jax.sharding import PartitionSpec as P

EPS = 1e-06
F32 = jnp.float32
BF16 = jnp.bfloat16
AXES = ("dp", "mp")
DEVICES = 128

Z_MASKS = (0, 1, 2, 3)
X_MASKS = (0, 4, 64, 68)
Y_MASKS = (0, 16, 32, 48)
CORE = 8
HALF_SEQ = 512
TOK = 128
CH = 384
WIDE = 768
CHUNKS = 8
STEPS = 64
GELU_A = 0.7978845608028654
GELU_B = 0.044715


def swap_send(values, mask):
    return lax.ppermute(values, AXES, [(i, i ^ mask) for i in range(DEVICES)])


def block_of(position, dp):
    mirrored = (position & 6) | ((position & 1) << 3) | ((position >> 3) & 1)
    return dp ^ mirrored


def gelu_parts(v):
    inner = GELU_A * (v + GELU_B * v * v * v)
    t = jnp.tanh(inner)
    half = 0.5 * (1.0 + t)
    slope = half + 0.5 * v * (1.0 - t * t) * (GELU_A * (1.0 + (3.0 * GELU_B) * v * v))
    return v * half, slope


def gelu_value(v):
    return v * (0.5 * (1.0 + jnp.tanh(GELU_A * (v + GELU_B * v * v * v))))


def neg_expm1(v):
    series = 1.0 + v * (1.0 / 9.0)
    for n in range(8, 1, -1):
        series = 1.0 + (v * (1.0 / n)) * series
    return jnp.where(v > -0.5, -v * series, 1.0 - jnp.exp(v))


def vmem(limit):
    return pltpu.CompilerParams(vmem_limit_bytes=limit * 1024 * 1024)


SMEM_SPEC = pl.BlockSpec(memory_space=pltpu.SMEM)


def block_rows(dp, p):
    return pl.ds(pl.multiple_of(block_of(p, dp) * 128, 128), 128)


def cols(p):
    return slice(p * 128, (p + 1) * 128)


def prep_kernel(scal, x_ref, g_ref, n_ref):
    dp = scal[2]
    x = x_ref[...].astype(F32)
    s = lax.rsqrt(jnp.mean(x * x, axis=-1, keepdims=True) + EPS)
    for p in range(16):
        src = block_rows(dp, p)
        n_ref[:, cols(p)] = (x_ref[:, src].astype(F32) * s * g_ref[:, src]).astype(BF16)


def prep(scal, x, g):
    return pl.pallas_call(
        prep_kernel,
        out_shape=jax.ShapeDtypeStruct((TOK, 2048), BF16),
        in_specs=[SMEM_SPEC] + [pl.BlockSpec(memory_space=pltpu.VMEM)] * 2,
        compiler_params=vmem(16),
        name="prep",
    )(scal, x, g)


def to_relative_kernel(scal, rows_ref, out0, out1):
    for p in range(16):
        out = (out0, out1)[p // 8]
        out[:, cols(p % 8)] = rows_ref[:, block_rows(scal[2], p)]


def to_relative(scal, rows):
    n = rows.shape[0]
    return pl.pallas_call(
        to_relative_kernel,
        grid=(2,),
        out_shape=(jax.ShapeDtypeStruct((n, 1024), rows.dtype),) * 2,
        in_specs=[SMEM_SPEC, pl.BlockSpec((n // 2, 2048), lambda i: (i, 0))],
        out_specs=(pl.BlockSpec((n // 2, 1024), lambda i: (i, 0)),) * 2,
        compiler_params=vmem(16),
        name="to_relative",
    )(scal, rows)


def gain_kernel(scal, in0, in1, out):
    for p in range(16):
        out[:, block_rows(scal[2], p)] = (in0, in1)[p // 8][:, cols(p % 8)]


def from_relative_gain(scal, g0, g1):
    return pl.pallas_call(
        gain_kernel,
        out_shape=jax.ShapeDtypeStruct((1, 2048), F32),
        in_specs=[SMEM_SPEC] + [pl.BlockSpec(memory_space=pltpu.VMEM)] * 2,
        name="gain_order",
    )(scal, g0, g1)


def assemble_kernel(scal, own, p1, p2_0, p2_1, p3, *outs):
    z = scal[0]
    for j, block in enumerate((own, p1, None, p3)):
        rows = pl.ds(pl.multiple_of((z ^ j) * TOK, TOK), TOK)
        for h in (0, 1):
            part = slice(h * 1024, (h + 1) * 1024)
            value = (p2_0, p2_1)[h][...] if block is None else block[:, part]
            if len(outs) == 2:
                outs[h][rows, :] = value
            else:
                outs[0][rows, part] = value


def assemble(scal, blocks, halves):
    shape = jax.ShapeDtypeStruct((HALF_SEQ, 1024 if halves else 2048), BF16)
    return pl.pallas_call(
        assemble_kernel,
        out_shape=(shape, shape) if halves else shape,
        in_specs=[SMEM_SPEC] + [pl.BlockSpec(memory_space=pltpu.VMEM)] * 5,
        compiler_params=vmem(16),
        name="assemble",
    )(scal, *blocks)


def add_blocks(dp, sums, base, out):
    own0, own1, a, b = sums
    for p in range(16):
        own = (own0, own1)[p // 8][:, cols(p % 8)]
        dst = block_rows(dp, p)
        total = own + a[:, cols(p)].astype(F32) + b[:, cols(p)].astype(F32)
        out[:, dst] = total if base is None else base[:, dst].astype(F32) + total


def mid_kernel(scal, x_ref, own0, own1, a, b, g_ref, xo_ref, n_ref):
    add_blocks(scal[2], (own0, own1, a, b), x_ref, xo_ref)
    x = xo_ref[...]
    s = lax.rsqrt(jnp.mean(x * x, axis=-1, keepdims=True) + EPS)
    n_ref[...] = (x * s * g_ref[...]).astype(BF16)


def mid_norm(scal, x, sums, g):
    return pl.pallas_call(
        mid_kernel,
        out_shape=(
            jax.ShapeDtypeStruct((TOK, 2048), F32),
            jax.ShapeDtypeStruct((TOK, 2048), BF16),
        ),
        in_specs=[SMEM_SPEC] + [pl.BlockSpec(memory_space=pltpu.VMEM)] * 6,
        compiler_params=vmem(16),
        name="mid_norm",
    )(scal, x, *sums, g)


def norm_gradient(x, g, dn):
    s = lax.rsqrt(jnp.mean(x * x, axis=-1, keepdims=True) + EPS)
    w = g * dn
    inner = jnp.mean(w * x, axis=-1, keepdims=True)
    return s * (w - x * (s * s * inner)), s


def back_two_kernel(scal, c_ref, x_ref, own0, own1, a, b, g_ref, dx_ref, dm_ref, dg_ref):
    own = jnp.concatenate([own0[...], own1[...]], axis=1)
    dn = own + a[...].astype(F32) + b[...].astype(F32)
    x = x_ref[...]
    back, s = norm_gradient(x, g_ref[...], dn)
    dg_ref[...] = jnp.sum(dn * x * s, axis=0, keepdims=True)
    dx_ref[...] = c_ref[...].astype(F32) + back
    for p in range(16):
        dm_ref[:, cols(p)] = dx_ref[:, block_rows(scal[2], p)].astype(BF16)


def norm_back_two(scal, c, x, sums, g):
    return pl.pallas_call(
        back_two_kernel,
        out_shape=(
            jax.ShapeDtypeStruct((TOK, 2048), F32),
            jax.ShapeDtypeStruct((TOK, 2048), BF16),
            jax.ShapeDtypeStruct((1, 2048), F32),
        ),
        in_specs=[SMEM_SPEC] + [pl.BlockSpec(memory_space=pltpu.VMEM)] * 7,
        compiler_params=vmem(24),
        name="norm_back_two",
    )(scal, c, x, *sums, g)


def back_one_kernel(scal, base_ref, x_ref, own0, own1, a, b, g_ref, dx_ref, dn_ref):
    add_blocks(scal[2], (own0, own1, a, b), None, dn_ref)
    back, _ = norm_gradient(x_ref[...].astype(F32), g_ref[...], dn_ref[...])
    dx_ref[...] = base_ref[...] + back


def norm_back_one(scal, base, x, sums, g):
    return pl.pallas_call(
        back_one_kernel,
        out_shape=jax.ShapeDtypeStruct((TOK, 2048), F32),
        in_specs=[SMEM_SPEC] + [pl.BlockSpec(memory_space=pltpu.VMEM)] * 7,
        scratch_shapes=[pltpu.VMEM((TOK, 2048), F32)],
        compiler_params=vmem(24),
        name="norm_back_one",
    )(scal, base, x, *sums, g)


PACK_ROWS = 16
ROW_CB, ROW_BR, ROW_BI, ROW_DECAY, ROW_MASK, ROW_H, ROW_SIG = 4, 5, 6, 7, 8, 9, 10


def row(ref, i):
    return ref[i : i + 1, :]


def valid_rows(scal, start, size):
    t = lax.broadcasted_iota(jnp.int32, (size, 1), 0) + (scal[1] * HALF_SEQ + start)
    return t < scal[3]


GROUPS = 3


def pack_kernel(sizes, cw, cb, br, bi, lam, h, cs, out):
    slot = lax.broadcasted_iota(jnp.int32, (1, CH), 1)
    limit = jnp.where(slot < 192, sizes[0], 192 + sizes[1])
    mask = jnp.where(slot < limit, 1.0, 0.0)
    out[...] = jnp.zeros_like(out)
    out[0:4, :] = cw[...]
    out[ROW_CB : ROW_CB + 1, :] = cb[...]
    out[ROW_BR : ROW_BR + 1, :] = br[...]
    out[ROW_BI : ROW_BI + 1, :] = bi[...]
    out[ROW_DECAY : ROW_DECAY + 1, :] = -8.0 * jax.nn.softplus(-lam[...])
    out[ROW_MASK : ROW_MASK + 1, :] = mask
    out[ROW_H : ROW_H + 1, :] = h[...] * mask
    out[ROW_SIG : ROW_SIG + 1, :] = jax.nn.sigmoid(-lam[...])
    out[11:14, :] = cs[...] * mask


def make_pack(head_sizes, *rows):
    return pl.pallas_call(
        pack_kernel,
        out_shape=jax.ShapeDtypeStruct((PACK_ROWS, CH), F32),
        in_specs=[SMEM_SPEC] + [pl.BlockSpec(memory_space=pltpu.VMEM)] * 7,
        name="pack",
    )(head_sizes, *rows)


def put(ref, rows, value):
    for g in range(GROUPS):
        ref[g, rows, :] = value[:, g * 128 : (g + 1) * 128]


def take(ref, rows):
    return jnp.concatenate([ref[g, rows, :] for g in range(GROUPS)], axis=1)


def at_step(ref, s):
    rows = pl.ds(s, CHUNKS, stride=STEPS)
    return [ref.at[g][rows, :] for g in range(GROUPS)]


def put_step(ref, s, values):
    rows = pl.ds(s, CHUNKS, stride=STEPS)
    for g in range(GROUPS):
        ref.at[g][rows, :] = values[g]


def run_steps(step):
    start = [jnp.zeros((CHUNKS, 128), F32)] * GROUPS + [jnp.ones((CHUNKS, 128), F32)] * GROUPS
    out = lax.fori_loop(0, STEPS, step, tuple(start), unroll=4)
    return jnp.concatenate(out[:GROUPS], axis=1), jnp.concatenate(out[GROUPS:], axis=1)


def mix_fwd_kernel(
    scal, pre_b, halo, par, wr, wi, rate, inlet, conv, xg, av, hl, pcum, ext, end, bv
):
    mask = row(par, ROW_MASK)
    ext[0:8, :] = halo[...]
    for c in range(CHUNKS):
        ext[8 + c * STEPS : 8 + (c + 1) * STEPS, :] = pre_b[c * STEPS : (c + 1) * STEPS, :] * mask
    for c in range(CHUNKS):
        t0 = c * STEPS
        acc = row(par, ROW_CB) + row(par, 0) * ext[t0 + 5 : t0 + 5 + STEPS, :]
        for k in range(1, 4):
            acc = acc + row(par, k) * ext[t0 + 5 + k : t0 + 5 + k + STEPS, :]
        acc = acc * mask
        conv[t0 : t0 + STEPS, :] = acc
        xg[t0 : t0 + STEPS, :] = acc.astype(BF16)
    rate[...] = jnp.dot(xg[...], wr[0], preferred_element_type=F32)
    inlet[...] = jnp.dot(xg[...], wi[0], preferred_element_type=F32)
    for c in range(CHUNKS):
        rows = slice(c * STEPS, (c + 1) * STEPS)
        r = jax.nn.sigmoid(rate[rows, :] + row(par, ROW_BR))
        i = jax.nn.sigmoid(inlet[rows, :] + row(par, ROW_BI))
        rate[rows, :] = r
        inlet[rows, :] = i
        log_a = row(par, ROW_DECAY) * r
        mult = jnp.sqrt(neg_expm1(2.0 * log_a))
        valid = valid_rows(scal, c * STEPS, STEPS)
        put(av, rows, jnp.where(valid, jnp.exp(log_a), 1.0))
        put(bv, rows, jnp.where(valid, mult * i * conv[rows, :], 0.0))

    def step(s, carry):
        a, b = at_step(av, s), at_step(bv, s)
        h = [a[g] * carry[g] + b[g] for g in range(GROUPS)]
        p = [a[g] * carry[GROUPS + g] for g in range(GROUPS)]
        put_step(hl, s, h)
        put_step(pcum, s, p)
        return tuple(h + p)

    h, p = run_steps(step)
    carry = row(par, ROW_H)
    for c in range(CHUNKS):
        carry = h[c : c + 1, :] + p[c : c + 1, :] * carry
    end[...] = jnp.broadcast_to(carry, (8, CH))


def wide(rows):
    return pl.BlockSpec((rows, CH), lambda i: (0, i))


GATE_SPEC = pl.BlockSpec((1, CH, CH), lambda i: (i, 0, 0))


STRIP_SPEC = pl.BlockSpec((GROUPS, 512, 128), lambda i: (i, 0, 0))
STRIP = jax.ShapeDtypeStruct((2 * GROUPS, 512, 128), F32)
STRIP_SCRATCH = pltpu.VMEM((GROUPS, 512, 128), F32)


def sds(rows, dtype=F32):
    return jax.ShapeDtypeStruct((rows, WIDE), dtype)


def mix_fwd(scal, pre_b, halo, par, wr, wi):
    return pl.pallas_call(
        mix_fwd_kernel,
        grid=(2,),
        out_shape=(
            sds(512), sds(512), sds(512), sds(512, BF16), STRIP, STRIP, STRIP, sds(520), sds(8),
        ),
        in_specs=[SMEM_SPEC, wide(512), wide(8), wide(16), GATE_SPEC, GATE_SPEC],
        out_specs=(
            wide(512), wide(512), wide(512), wide(512), STRIP_SPEC, STRIP_SPEC, STRIP_SPEC, wide(520), wide(8),
        ),
        scratch_shapes=[STRIP_SCRATCH],
        compiler_params=vmem(32),
        name="mix_fwd",
    )(scal, pre_b, halo, par, wr, wi)


def mix_out_kernel(scal, hl, pcum, pre_a, h_in, h_ext, mixed, final):
    h_ext[0:8, :] = h_in[...]
    carry = row(h_in, 7)
    for c in range(CHUNKS):
        rows = slice(c * STEPS, (c + 1) * STEPS)
        h = take(hl, rows) + take(pcum, rows) * carry
        h_ext[8 + c * STEPS : 8 + (c + 1) * STEPS, :] = h
        carry = h[STEPS - 1 : STEPS, :]
        mixed[rows, :] = (gelu_value(pre_a[rows, :]) * h).astype(BF16)
    final[...] = jnp.broadcast_to(carry, (8, CH))


def mix_out(scal, hl, pcum, pre_a, h_in):
    return pl.pallas_call(
        mix_out_kernel,
        grid=(2,),
        out_shape=(sds(520), sds(512, BF16), sds(8)),
        in_specs=[SMEM_SPEC, STRIP_SPEC, STRIP_SPEC, wide(512), wide(8)],
        out_specs=(wide(520), wide(512), wide(8)),
        compiler_params=vmem(32),
        name="mix_out",
    )(scal, hl, pcum, pre_a, h_in)


def mix_back_kernel(scal, d_mix, pre_a, h_ext, av, d_pre_a, rl, qcum, end, dh):
    for c in range(CHUNKS):
        rows = slice(c * STEPS, (c + 1) * STEPS)
        act, slope = gelu_parts(pre_a[rows, :])
        dm = d_mix[rows, :]
        h = h_ext[8 + c * STEPS : 8 + (c + 1) * STEPS, :]
        d_pre_a[rows, :] = (slope * h * dm).astype(BF16)
        put(dh, rows, dm * act)

    def step(n, carry):
        s = STEPS - 1 - n
        a, d = at_step(av, s), at_step(dh, s)
        carried = [d[g] + carry[g] for g in range(GROUPS)]
        put_step(rl, s, carried)
        put_step(qcum, s, carry[GROUPS:])
        u = [a[g] * carried[g] for g in range(GROUPS)]
        return tuple(u + [a[g] * carry[GROUPS + g] for g in range(GROUPS)])

    u, q = run_steps(step)
    carry = jnp.zeros((1, CH), F32)
    for c in range(CHUNKS - 1, -1, -1):
        carry = u[c : c + 1, :] + q[c : c + 1, :] * carry
    end[...] = jnp.broadcast_to(carry, (8, CH))


def mix_back(scal, d_mix, pre_a, h_ext, av):
    return pl.pallas_call(
        mix_back_kernel,
        grid=(2,),
        out_shape=(sds(512, BF16), STRIP, STRIP, sds(8)),
        in_specs=[SMEM_SPEC, wide(512), wide(512), wide(520), STRIP_SPEC],
        out_specs=(wide(512), STRIP_SPEC, STRIP_SPEC, wide(8)),
        scratch_shapes=[STRIP_SCRATCH],
        compiler_params=vmem(32),
        name="mix_back",
    )(scal, d_mix, pre_a, h_ext, av)


def total_rows(v):
    return jnp.sum(v, axis=0, keepdims=True)


def mix_grad_kernel(
    scal, rl, qcum, av, u_in, rate, inlet, conv, h_ext, ext, par, wr, wi,
    d_pre_r, d_pre_i, d_pre_b, tail, head, sums, dconv,
):
    mask = row(par, ROW_MASK)
    carry = row(u_in, 0)
    d_lam = jnp.zeros((1, CH), F32)
    d_br = jnp.zeros((1, CH), F32)
    d_bi = jnp.zeros((1, CH), F32)
    for c in range(CHUNKS - 1, -1, -1):
        t0 = c * STEPS
        rows = slice(t0, t0 + STEPS)
        a = take(av, rows)
        carried = take(rl, rows) + take(qcum, rows) * carry
        carry = a[0:1, :] * carried[0:1, :]
        valid = valid_rows(scal, t0, STEPS)
        d_drive = jnp.where(valid, carried, 0.0)
        d_decay = d_drive * h_ext[t0 + 7 : t0 + 7 + STEPS, :]
        r, i, x = rate[rows, :], inlet[rows, :], conv[rows, :]
        gap = neg_expm1(2.0 * (row(par, ROW_DECAY) * r))
        inv = lax.rsqrt(gap)
        mult = gap * inv
        driven = d_drive * i
        d_log = d_decay * a - driven * x * (a * a) * inv
        d_lam = d_lam + total_rows(d_log * r)
        pr = (d_log * row(par, ROW_DECAY) * r * (1.0 - r)).astype(BF16)
        pi = (d_drive * mult * x * i * (1.0 - i)).astype(BF16)
        d_pre_r[rows, :] = pr
        d_pre_i[rows, :] = pi
        d_br = d_br + total_rows(pr.astype(F32))
        d_bi = d_bi + total_rows(pi.astype(F32))
        dconv[rows, :] = driven * mult
    dims = (((1,), (1,)), ((), ()))
    gate = lax.dot_general(d_pre_r[...], wr[0], dims, preferred_element_type=F32)
    gate = gate + lax.dot_general(d_pre_i[...], wi[0], dims, preferred_element_type=F32)
    dconv[0:HALF_SEQ, :] = (dconv[0:HALF_SEQ, :] + gate) * mask
    dconv[HALF_SEQ : HALF_SEQ + 8, :] = jnp.zeros((8, CH), F32)
    head[...] = dconv[0:8, :]
    taps = [jnp.zeros((1, CH), F32) for _ in range(4)]
    bias = jnp.zeros((1, CH), F32)
    for c in range(CHUNKS):
        t0 = c * STEPS
        here = dconv[t0 : t0 + STEPS, :]
        bias = bias + total_rows(here)
        back = jnp.zeros((STEPS, CH), F32)
        for k in range(4):
            taps[k] = taps[k] + total_rows(here * ext[t0 + 5 + k : t0 + 5 + k + STEPS, :])
            back = back + row(par, k) * dconv[t0 + 3 - k : t0 + 3 - k + STEPS, :]
        back = back * mask
        d_pre_b[t0 : t0 + STEPS, :] = back.astype(BF16)
        if c == CHUNKS - 1:
            tail[...] = back[STEPS - 16 :, :]
    for k in range(4):
        sums[k : k + 1, :] = taps[k]
    sums[4:5, :] = bias
    sums[5:6, :] = d_br
    sums[6:7, :] = d_bi
    sums[7:8, :] = 8.0 * row(par, ROW_SIG) * d_lam


def mix_grad(scal, rl, qcum, av, u_in, rate, inlet, conv, h_ext, ext, par, wr, wi):
    return pl.pallas_call(
        mix_grad_kernel,
        grid=(2,),
        out_shape=(sds(512, BF16), sds(512, BF16), sds(512, BF16), sds(16), sds(8), sds(8)),
        in_specs=[
            SMEM_SPEC, STRIP_SPEC, STRIP_SPEC, STRIP_SPEC, wide(8), wide(512), wide(512), wide(512),
            wide(520), wide(520), wide(16), GATE_SPEC, GATE_SPEC,
        ],
        out_specs=(wide(512), wide(512), wide(512), wide(16), wide(8), wide(8)),
        scratch_shapes=[pltpu.VMEM((HALF_SEQ + 8, CH), F32)],
        compiler_params=vmem(40),
        name="mix_grad",
    )(scal, rl, qcum, av, u_in, rate, inlet, conv, h_ext, ext, par, wr, wi)


def tie(values, *earlier):
    return lax.optimization_barrier((values, earlier))[0]


def gather_z(own):
    p1 = swap_send(own, 1)
    p3 = swap_send(own, 3)
    p2_0 = swap_send(p3[:, :1024], 1)
    p2_1 = swap_send(p1[:, 1024:], 3)
    return own, p1, p2_0, p2_1, p3


def far_blocks(z, part0, part1):
    return [
        lax.dynamic_slice_in_dim(p, (z ^ 2) * TOK, TOK, 0).astype(BF16) for p in (part0, part1)
    ]


def scatter_z(z, part0, part1, far=None):
    def block(part, j):
        return lax.dynamic_slice_in_dim(part, (z ^ j) * TOK, TOK, 0)

    far = far or far_blocks(z, part0, part1)
    far_0 = swap_send(far[0], 1)
    far_1 = swap_send(far[1], 3)
    to_1 = [block(part0, 1).astype(BF16), (block(part1, 1) + far_1.astype(F32)).astype(BF16)]
    to_3 = [(block(part0, 3) + far_0.astype(F32)).astype(BF16), block(part1, 3).astype(BF16)]
    r1 = swap_send(jnp.concatenate(to_1, axis=1), 1)
    r3 = swap_send(jnp.concatenate(to_3, axis=1), 3)
    return block(part0, 0), block(part1, 0), r1, r3


Z_GROUPS = [[0, 1, 2, 3], [4, 5, 6, 7]]


def reduce_z(values):
    return lax.psum_scatter(
        values, "mp", scatter_dimension=0, axis_index_groups=Z_GROUPS, tiled=True
    )


def cross(axis, blocks):
    return jnp.concatenate(
        [
            jnp.concatenate([blocks[0], blocks[1]], axis=-1),
            jnp.concatenate([blocks[2], blocks[3]], axis=-1),
        ],
        axis=axis,
    )


def join_mixer_kernel(*refs):
    one, two, out = refs[:4], refs[4:8], refs[8]
    for y in range(4):
        rows = slice(y * 256, (y + 1) * 256)
        out[rows, :CH] = one[y][:, :CH]
        out[rows, CH:WIDE] = one[y][:, 512 : 512 + CH]
        out[rows, 2 * WIDE : 2 * WIDE + 128] = one[y][:, CH:512]
        out[rows, 2 * WIDE + CH : 2 * WIDE + CH + 128] = one[y][:, 512 + CH :]
        for r in (0, 1):
            rows = slice(y * 256 + r * 128, y * 256 + (r + 1) * 128)
            own, other = two[2 * r], two[2 * r + 1]
            out[rows, WIDE : WIDE + CH] = own[y, :, :CH]
            out[rows, WIDE + CH : 2 * WIDE] = other[y, :, :CH]
            out[rows, 2 * WIDE + 128 : 2 * WIDE + CH] = own[y, :, CH:]
            out[rows, 2 * WIDE + CH + 128 :] = other[y, :, CH:]


def join_mixer(one, two):
    return pl.pallas_call(
        join_mixer_kernel,
        out_shape=jax.ShapeDtypeStruct((1024, 3 * WIDE), BF16),
        compiler_params=vmem(24),
        name="join_mixer",
    )(*one, *two)


def sum_four(own, a, b, c):
    return (own.astype(F32) + a.astype(F32)) + (b.astype(F32) + c.astype(F32))


def add_low(a, b):
    return (a.astype(F32) + b.astype(F32)).astype(BF16)


def y_pieces(total):
    return [total[k * 256 : (k + 1) * 256] for k in range(4)]


def x_pieces(total):
    n = total.shape[-1] // 2
    return [total[:, r * 128 : (r + 1) * 128, c * n : (c + 1) * n] for r in (0, 1) for c in (0, 1)]


def send_three(pieces, masks):
    return [swap_send(v, m) for v, m in zip(pieces[1:], masks[1:])]


def first_y(total):
    py = y_pieces(total)
    received = send_three(py, Y_MASKS)
    pieces = [v[0] for v in x_pieces(sum_four(py[0], *received).astype(BF16)[None])]
    return received, pieces, X_MASKS


def first_x(total):
    px = x_pieces(total.reshape(4, 256, -1))
    received = send_three(px, X_MASKS)
    total = sum_four(px[0], *received).astype(BF16)
    return received, [total[k] for k in range(4)], Y_MASKS


def finish_kernel(*refs, turned):
    total = sum_four(*[r[...] for r in refs[:4]])
    at = 0
    for out, turn in zip(refs[4:], turned):
        n = out.shape[0] if turn else out.shape[1]
        part = total[:, at : at + n]
        out[...] = part.T if turn else part
        at += n


def finish(stage, *turned):
    _, pieces, masks = stage
    terms = [pieces[0]] + send_three(pieces, masks)
    n = pieces[0].shape[1] // len(turned)
    shapes = [jax.ShapeDtypeStruct((n, TOK) if t else (TOK, n), F32) for t in turned]
    return pl.pallas_call(
        functools.partial(finish_kernel, turned=turned),
        out_shape=tuple(shapes),
        compiler_params=vmem(16),
        name="finish",
    )(*terms)


def outer_mlp_kernel(n_ref, c_ref, gu_ref, h_ref, out_ref, turned):
    step = pl.program_id(0)

    @pl.when(step == 0)
    def _():
        turned[...] = n_ref[...].T

    @pl.when(step == 6)
    def _():
        turned[...] = c_ref[...].T

    @pl.when(step < 6)
    def _():
        out_ref[...] = jnp.dot(turned[...], gu_ref[...], preferred_element_type=F32).astype(BF16)

    @pl.when(step >= 6)
    def _():
        out_ref[...] = jnp.dot(turned[...], h_ref[...], preferred_element_type=F32).astype(BF16)


def outer_mlp(rows_two, rows_c, d_gate_up, hidden):
    whole = pl.BlockSpec((HALF_SEQ, 2048), lambda i: (0, 0))
    return pl.pallas_call(
        outer_mlp_kernel,
        grid=(9,),
        out_shape=jax.ShapeDtypeStruct((2048, 6 * WIDE), BF16),
        in_specs=[
            whole,
            whole,
            pl.BlockSpec((HALF_SEQ, 512), lambda i: (0, jnp.minimum(i, 5))),
            pl.BlockSpec((HALF_SEQ, 512), lambda i: (0, jnp.maximum(i - 6, 0))),
        ],
        out_specs=pl.BlockSpec((2048, 512), lambda i: (0, i)),
        scratch_shapes=[pltpu.VMEM((2048, HALF_SEQ), BF16)],
        compiler_params=vmem(40),
        cost_estimate=pl.CostEstimate(
            flops=2 * 2048 * 4608 * 512, bytes_accessed=30 * 2**20, transcendentals=0
        ),
        name="outer_mlp",
    )(rows_two, rows_c, d_gate_up, hidden)


def finish_mlp_kernel(mine, other, gate, up, down):
    for k, out in enumerate((gate, up)):
        own = mine[:, 2 * k * WIDE : (2 * k + 1) * WIDE]
        out[...] = own.astype(F32) + other[:, k * WIDE : (k + 1) * WIDE].astype(F32)
    own = mine[:, 4 * WIDE : 5 * WIDE]
    down[...] = (own.astype(F32) + other[:, 2 * WIDE :].astype(F32)).T


def send_mlp(shards):
    given = [shards[:, k * WIDE : (k + 1) * WIDE] for k in (1, 3, 5)]
    return swap_send(jnp.concatenate(given, axis=1), 4)


def finish_mlp(shards, received):
    shape = jax.ShapeDtypeStruct((TOK, WIDE), F32)
    return pl.pallas_call(
        finish_mlp_kernel,
        out_shape=(shape, shape, jax.ShapeDtypeStruct((WIDE, TOK), F32)),
        compiler_params=vmem(16),
        name="finish_mlp",
    )(shards, received)


def swap_channels(v):
    return jnp.concatenate([v[..., CH:], v[..., :CH]], axis=-1)


def dot(a, b):
    return jnp.dot(a, b, preferred_element_type=F32)


def dot_back(a, b):
    return lax.dot_general(a, b, (((1,), (1,)), ((), ())), preferred_element_type=F32)


def dot_outer(a, b):
    return lax.dot_general(a, b, (((0,), (0,)), ((), ())), preferred_element_type=F32)


def pair_blocks(w):
    zero = jnp.zeros_like(w[..., 0, :, :])
    top = jnp.concatenate([w[..., 0, :, :], zero], axis=-1)
    low_rows = jnp.concatenate([zero, w[..., 1, :, :]], axis=-1)
    return jnp.concatenate([top, low_rows], axis=-2)


def on_device(
    inputs,
    lengths,
    head_sizes,
    h_start,
    conv_start,
    g_one,
    w_a,
    w_b,
    conv_w,
    conv_b,
    w_r,
    w_i,
    b_r,
    b_i,
    lam,
    w_out,
    g_two,
    w_gate,
    w_up,
    w_down,
    cotangent,
):
    dp = lax.axis_index("dp").astype(jnp.int32)
    mp = lax.axis_index("mp").astype(jnp.int32)
    z, x_lo, core = mp % 4, mp // 4, dp % 2
    length = lengths[0]
    scal = jnp.stack([z, x_lo, dp, length])
    first_half = x_lo == 0
    g_one, g_two = g_one[None], g_two[None]

    shard = jnp.concatenate([w_gate, w_up, w_down.T], axis=1)

    out_t = w_out.T
    first = jnp.concatenate([w_a, out_t[:, :128]], axis=1)
    second = jnp.concatenate([w_b, out_t[:, 128:]], axis=1)
    gates = jnp.stack([w_r, w_i])
    y1, y3 = swap_send(second, 16), swap_send(second, 48)
    x3, x1 = swap_send(first, 68), swap_send(first, 4)
    x = inputs[0]
    c = cotangent[0]
    pack = make_pack(
        head_sizes, conv_w, conv_b[None], b_r[None], b_i[None], lam[None], h_start, conv_start[0]
    )
    pair = jnp.concatenate([shard, gates.reshape(TOK, 1152)], axis=1)
    far_first, far_second, pair = tie((first, second, pair), y1, y3, x1, x3)
    x2, y2 = swap_send(far_first, 64), swap_send(far_second, 32)
    pair = swap_send(pair, 4)
    n_one = tie(prep(scal, x, g_one), y1, y3, x1, x3)
    z1, z3 = swap_send(n_one, 1), swap_send(n_one, 3)
    pair = tie(pair, z1, z3)
    pack_other = swap_send(tie(pack, pair), 4)
    other, gates_other = pair[:, :2304], pair[:, 2304:]
    shard = jnp.concatenate(
        [v[:, i * WIDE : (i + 1) * WIDE] for i in range(3) for v in (shard, other)], axis=1
    )
    w_mlp = lax.all_gather(shard, "dp", axis=0, tiled=True)

    par = jnp.concatenate([pack, pack_other], axis=1)
    gates = pair_blocks(jnp.stack([gates, gates_other.reshape(gates.shape)], axis=1))
    wr, wi = gates[0], gates[1]
    rows = cross(0, [first, x1, x2, x3])
    stack = jnp.stack([second, y1, y2, y3], axis=0)
    rows, stack = tie((rows, stack), n_one, pack_other)
    ry1, ry3, sx2 = swap_send(rows, 16), swap_send(rows, 48), swap_send(stack, 64)
    z2_0, z2_1 = swap_send(z3[:, :1024], 1), swap_send(z1[:, 1024:], 3)
    far_rows, far_stack = tie((rows, stack), ry1, ry3, sx2, z1, z3)
    ry2, sx1, sx3 = swap_send(far_rows, 32), swap_send(far_stack, 4), swap_send(far_stack, 68)
    c_sent = tie(c, z1, z3)
    c1, c3 = swap_send(c_sent, 1), swap_send(c_sent, 3)
    ry2, sx1, sx3 = tie((ry2, sx1, sx3), z2_0, z2_1, c1, c3)
    mixer = join_mixer((rows, ry1, ry2, ry3), (stack, sx1, sx2, sx3))
    rows_one = assemble(scal, (n_one, z1, z2_0, z2_1, z3), True)
    mixers = (mixer, swap_send(mixer, CORE))
    wa = [m[:, :WIDE] for m in mixers]
    wb = [m[:, WIDE : 2 * WIDE] for m in mixers]
    wo = [m[:, 2 * WIDE :] for m in mixers]

    pre_b = dot(rows_one[0], wb[0]) + dot(rows_one[1], wb[1])
    edge = swap_channels(swap_send(pre_b[HALF_SEQ - 8 :], 4)) * par[ROW_MASK : ROW_MASK + 1]
    start_halo = jnp.concatenate([jnp.zeros((5, WIDE), F32), par[11:14]], axis=0)
    halo = jnp.where(first_half, start_halo, edge)
    par_used = par.at[ROW_H].set(jnp.where(first_half, par[ROW_H], 0.0))
    pre_a = dot(rows_one[0], wa[0]) + dot(rows_one[1], wa[1])
    rate, inlet, conv, xg, av, hl, pcum, ext, end = mix_fwd(scal, pre_b, halo, par_used, wr, wi)
    arrived = swap_channels(swap_send(end, 4))
    h_in = jnp.where(first_half, jnp.broadcast_to(par[ROW_H : ROW_H + 1], (8, WIDE)), arrived)
    c3_sent, c1_sent = tie((c3[:, :1024], c1[:, 1024:]), rows_one[0])
    c2_0, c2_1 = swap_send(c3_sent, 1), swap_send(c1_sent, 3)
    h_in = tie(h_in, c2_0, c2_1)
    h_ext, mixer_in, final = mix_out(scal, hl, pcum, pre_a, h_in)
    sums = scatter_z(z, dot_back(mixer_in, wo[0]), dot_back(mixer_in, wo[1]))
    rows_c = assemble(scal, (c, c1, c2_0, c2_1, c3), False)
    x_one, n_two = mid_norm(scal, x, sums, g_two)

    w_gate_up, w_dn = w_mlp[:, : 4 * WIDE], w_mlp[:, 4 * WIDE :]
    rows_two = assemble(scal, gather_z(n_two), False)
    gate_up = dot(rows_two, w_gate_up)
    d_hidden = dot(rows_c, w_dn)
    gate_pre, up_pre = gate_up[:, : 2 * WIDE], gate_up[:, 2 * WIDE :]
    act, slope = gelu_parts(gate_pre)
    hidden = (act * up_pre).astype(BF16)
    d_gate = (slope * (up_pre * d_hidden)).astype(BF16)
    d_up = (act * d_hidden).astype(BF16)
    d_gate_up = jnp.concatenate([d_gate, d_up], axis=1)
    d_rows = dot_back(d_gate_up, w_gate_up)
    d_rows = [d_rows[:, :1024], d_rows[:, 1024:]]
    far = far_blocks(z, *d_rows)
    d_w_mlp = outer_mlp(rows_two, rows_c, tie(d_gate_up, *d_rows), hidden)
    shards = lax.psum_scatter(d_w_mlp, "dp", scatter_dimension=0, tiled=True)
    sums = scatter_z(z, d_rows[0], d_rows[1], far)
    d_x_one, dm, d_g_two = norm_back_two(scal, c, x_one, sums, g_two)

    def outer_core(rows, grads):
        given, mine = [dot_outer(rows[h], grads).astype(BF16) for h in (1, 0)]
        return mine, swap_send(given, CORE)

    d_result = dot_back(tie(hidden, d_w_mlp), w_dn).astype(BF16)
    dm = tie(dm, d_result)

    rows_m = list(assemble(scal, gather_z(dm), True))
    d_mix = dot(rows_m[0], wo[0]) + dot(rows_m[1], wo[1])
    d_pre_a, rl, qcum, end = mix_back(scal, d_mix, pre_a, h_ext, av)
    arrived = swap_channels(swap_send(end, 4))
    u_in = jnp.where(first_half, arrived, 0.0)

    def own_first(o, a):
        return jnp.concatenate([o[:, :CH], a[:, :CH], o[:, CH:], a[:, CH:]], axis=1)

    oa = [
        own_first(
            dot_outer(rows_m[h], mixer_in).astype(BF16), dot_outer(rows_one[h], d_pre_a).astype(BF16)
        )
        for h in (0, 1)
    ]
    oa[1] = swap_send(oa[1], CORE)
    u_in = tie(u_in, oa[1])
    total_oa = add_low(*oa)
    oa = first_y(total_oa)
    d_pre_r, d_pre_i, d_pre_b, tail, head, sums8 = mix_grad(
        scal, rl, qcum, av, u_in, rate, inlet, conv, h_ext, ext, par, wr, wi
    )
    d_result = reduce_z(tie(d_result, head))
    result = (x_one + d_result.astype(F32)).astype(BF16)
    after = jnp.where(first_half, swap_channels(swap_send(head, 4)), 0.0)[:3]
    ahead = jnp.concatenate([jnp.zeros((16, WIDE), F32), after], axis=0)
    extra = par[0:1] * ahead[3:19]
    for k in range(1, 4):
        extra = extra + par[k : k + 1] * ahead[3 - k : 19 - k]
    tail = (tail + extra * par[ROW_MASK : ROW_MASK + 1]).astype(BF16)
    d_pre_b = lax.dynamic_update_slice_in_dim(d_pre_b, tail, HALF_SEQ - 16, 0)

    d_pre_b = tie(d_pre_b, total_oa)
    d_rows = [dot_back(d_pre_a, wa[h]) + dot_back(d_pre_b, wb[h]) for h in (0, 1)]
    sums = scatter_z(z, d_rows[0], d_rows[1])
    d_inputs = norm_back_one(scal, d_x_one, x, sums, g_one)
    d_g_one = [
        jnp.sum(d_rows[h] * rows_one[h].astype(F32), axis=0, keepdims=True) for h in (0, 1)
    ]
    d_g_one = from_relative_gain(scal, *d_g_one) / g_one

    def gate_grads(k):
        part = slice(k * CH, (k + 1) * CH)
        both = [dot_outer(xg[:, part], g[:, part]) for g in (d_pre_r, d_pre_i)]
        return jnp.stack([v[q : q + 192, q : q + 192] for v in both for q in (0, 192)])

    def small_rows(k):
        return jnp.concatenate(
            [
                gate_grads(k).reshape(2, 192, CH),
                sums8[:, k * CH : (k + 1) * CH].reshape(2, 4, CH),
                gain_rows,
            ],
            axis=1,
        ).astype(BF16)

    gains = jnp.concatenate([d_g_one, d_g_two], axis=0)
    for mask in (1, 2):
        gains = gains + swap_send(gains, mask)
    gains = gains.reshape(-1)
    gain_rows = jnp.concatenate([gains, jnp.zeros((4608 - 4096,), F32)]).reshape(2, 6, CH)
    small = jnp.stack([small_rows(0), small_rows(1)], axis=1)
    kept = lax.dynamic_index_in_dim(small, core, 0, keepdims=False)
    given = lax.dynamic_index_in_dim(small, 1 - core, 0, keepdims=False)

    kept = add_low(kept, swap_send(given, CORE))
    total_b = add_low(*outer_core(rows_one, tie(d_pre_b, small)))
    kept = tie(kept, total_b, *oa[0], *sums)
    kept = add_low(kept[0], swap_send(kept[1], 4))
    b_stage = first_y(total_b)
    received = send_mlp(tie(shards, kept))
    d_w_gate, d_w_up, d_w_down = finish_mlp(shards, received)
    kept = add_low(kept, swap_send(kept, 64))
    oa = (oa[0], tie(oa[1], kept), oa[2])
    d_w_out, d_w_a = finish(oa, True, False)
    kept = tie(kept, *b_stage[0])
    kept = add_low(kept, swap_send(kept, 16))
    kept = tie(kept, received)
    kept = add_low(kept, swap_send(kept, 32))
    (d_w_b,) = finish((b_stage[0], tie(b_stage[1], kept), b_stage[2]), False)
    back = swap_send(kept, CORE)
    small = jnp.where(core == 0, jnp.stack([kept, back]), jnp.stack([back, kept])).astype(F32)
    d_gates = small[:, :192].reshape(2, 2, 192, 192)
    sums8 = small[:, 192:196].reshape(8, CH)
    gains = small[:, 196:].reshape(-1)[:4096].reshape(2, 2048)

    in_second = (length > HALF_SEQ).astype(jnp.int32)
    window = lax.dynamic_slice_in_dim(ext, 5 + jnp.clip(length - HALF_SEQ * x_lo, 0, HALF_SEQ), 3, 0)
    window = jnp.where(x_lo == in_second, window, 0.0)
    state = jnp.where(first_half, 0.0, final[:1])
    ends = tie(jnp.concatenate([window, state], axis=0), received)
    ends = ends[:, :CH] + swap_send(ends[:, CH:], 4)

    return (
        result[None],
        ends[3:4],
        ends[None, :3],
        d_inputs[None],
        gains[0],
        d_w_a,
        d_w_b,
        sums8[0:4],
        sums8[4],
        d_gates[0],
        d_gates[1],
        sums8[5],
        sums8[6],
        sums8[7],
        d_w_out,
        gains[1],
        d_w_gate,
        d_w_up,
        d_w_down,
    )


def solution(mesh):
    return jax.shard_map(
        on_device,
        mesh=mesh,
        in_specs=(
            P("dp", "mp", None),
            P("dp"),
            P("mp"),
            P("dp", "mp"),
            P("dp", None, "mp"),
            P(),
            P("dp", "mp"),
            P("dp", "mp"),
            P(None, "mp"),
            P("mp"),
            P("mp", None, None),
            P("mp", None, None),
            P("mp"),
            P("mp"),
            P("mp"),
            P("mp", "dp"),
            P(),
            P("dp", "mp"),
            P("dp", "mp"),
            P("mp", "dp"),
            P("dp", "mp", None),
        ),
        out_specs=(
            P("dp", "mp", None),
            P("dp", "mp"),
            P("dp", None, "mp"),
            P("dp", "mp", None),
            P(),
            P("dp", "mp"),
            P("dp", "mp"),
            P(None, "mp"),
            P("mp"),
            P("mp", None, None),
            P("mp", None, None),
            P("mp"),
            P("mp"),
            P("mp"),
            P("mp", "dp"),
            P(),
            P("dp", "mp"),
            P("dp", "mp"),
            P("mp", "dp"),
        ),
        check_vma=False,
    )
```
